256 devices in a mesh: dom: 32 (over z, x), grp: 8 (over y, core).
Axes of the slice: x: 4, y: 4, z: 8, core: 2. Of those that a mesh axis runs over, the one named last changes fastest.
Arguments:
- heads: int32 [2097152], P(('dom', 'grp')), may hold values from 0 to 4095
- tails: int32 [2097152], P(('dom', 'grp')), may hold values from 0 to 8191, as said below
- signs: int32 [2, 2097152], P(None, ('dom', 'grp')), may hold values from 0 to 4095
- edge_weights: float32 [2097152], P(('dom', 'grp')), may hold values from 0.25 to 4
- ground: float32 [131072], P(('dom', 'grp')), may hold values from 2 to 40
Outputs:
- solution: float32 [24, 131072], P(None, ('dom', 'grp'))
- residual: float32 [24, 131072], P(None, ('dom', 'grp'))
The draws below stay inside these ranges and needn't reach their ends.
Inputs may be any that keep to these rules, and one draw needn't show every extreme that they name: `tails`: every second endpoint is a vertex of the graph.
All inputs are finite; a program needn't handle non-finite values.
Results may differ from the reference program's by a relative error of at most 0.0003.
Values sent between devices are 32-bit elements; how exact they have to be, the bound alone decides.
A program may use at most 64 MiB of HBM per device.

```python
import math
import jax
import jax.numpy as jnp
from jax import lax

K = 24
ITERS = 3
DOMAIN = 4096
REACH = 2048
EDEV = 8192
EDOM = 65536
DOMAINS = 32
VERTS = 131072
EDGES = 2097152


def draw_heads(key, part):
    key = jax.random.fold_in(key, 11)
    values = jax.random.randint(key, (EDGES,), 0, DOMAIN, dtype=jnp.int32)
    position = jnp.arange(EDGES, dtype=jnp.int32) % EDEV
    values = jnp.where(position == 2, DOMAIN - 1, values)
    return jnp.where(position == 3, 0, values).astype(jnp.int32)


def draw_tails(key, part):
    key = jax.random.fold_in(key, 23)
    index = jnp.arange(EDGES, dtype=jnp.int32)
    domain_of = index // EDOM
    lowest = jnp.where(domain_of == 0, REACH, 0).astype(jnp.int32)
    highest = jnp.where(domain_of == DOMAINS - 1, DOMAIN + REACH, 2 * DOMAIN).astype(jnp.int32)
    values = jax.random.randint(key, (EDGES,), lowest, highest, dtype=jnp.int32)
    position = index % EDEV
    values = jnp.where(position == 0, lowest, values)
    return jnp.where(position == 1, highest - 1, values).astype(jnp.int32)


def draw_signs(key, part):
    key = jax.random.fold_in(key, 37)
    values = jax.random.randint(key, (2, EDGES), 0, 4096, dtype=jnp.int32)
    position = jnp.arange(EDGES, dtype=jnp.int32) % EDEV
    values = jnp.where(position[None, :] == 0, 4095, values)
    return jnp.where(position[None, :] == 1, 0, values).astype(jnp.int32)


def block_levels(own_key, shape, pieces, smallest, largest):
    factor_of, own = 1.0, jax.random.fold_in(own_key, 6)
    for axis_at, shards_of in pieces:
        steps = jnp.exp(jax.random.uniform(jax.random.fold_in(own, axis_at), (shards_of,), jnp.float32, smallest / len(pieces), largest / len(pieces)))
        factor_of = factor_of * jnp.repeat(steps, shape[axis_at] // shards_of).reshape([-1 if axis == axis_at else 1 for axis in range(len(shape))])
    return factor_of


def setup_inputs(seed: int = 0) -> dict:
    key_of = jax.random.split(jax.random.key(seed), 6)
    return {
        "heads": draw_heads(jax.random.fold_in(key_of[5], 71), 0),
        "tails": draw_tails(jax.random.fold_in(key_of[5], 71), 0),
        "signs": draw_signs(jax.random.fold_in(key_of[5], 71), 0),
        "edge_weights": jnp.clip(jnp.exp(math.log(4.0) - 2.7725887 * jax.random.uniform(key_of[3], (EDGES,), jnp.float32) ** block_levels(key_of[3], (EDGES,), ((0, 256),), -0.2, 0.2)), 0.25, 4.0),
        "ground": jnp.clip(jnp.exp(math.log(40.0) - 2.9957323 * jax.random.uniform(key_of[4], (VERTS,), jnp.float32) ** block_levels(key_of[4], (VERTS,), ((0, 256),), -0.2, 0.2)), 2.0, 40.0),
    }


def unpack(signs):
    half = K // 2
    shifts = jnp.arange(half, dtype=jnp.int32)
    bits = jnp.right_shift(signs[:, None, :], shifts[None, :, None]) & 1
    return (2 * bits - 1).reshape(2 * half, -1).astype(jnp.float32)

def reference(heads, tails, signs, edge_weights, ground):
    domain_of = jnp.arange(EDGES, dtype=jnp.int32) // EDOM
    start = (domain_of * DOMAIN).astype(jnp.int32)
    first = (start + heads).astype(jnp.int32)
    second = (start - REACH + tails).astype(jnp.int32)
    blocks = EDGES // EDEV
    first_b = first.reshape(blocks, EDEV)
    second_b = second.reshape(blocks, EDEV)
    weight_b = edge_weights.reshape(blocks, EDEV)
    signs_b = jnp.transpose(signs.reshape(2, blocks, EDEV), (1, 0, 2))

    def sketch_step(acc, block):
        head_idx, tail_idx, weight, sign_words = block
        scaled = unpack(sign_words) * jnp.sqrt(weight)[None, :]
        plus = jnp.concatenate([scaled, weight[None, :]], axis=0)
        minus = jnp.concatenate([-scaled, weight[None, :]], axis=0)
        return (acc.at[:, head_idx].add(plus).at[:, tail_idx].add(minus), None)
    start_acc = jnp.zeros((K + 1, VERTS), jnp.float32)
    gathered, _ = lax.scan(sketch_step, start_acc, (first_b, second_b, weight_b, signs_b))
    right = gathered[:K]
    diag = gathered[K] + ground

    def operate(field):

        def step(acc, block):
            head_idx, tail_idx, weight = block
            diff = weight[None, :] * (field[:, head_idx] - field[:, tail_idx])
            return (acc.at[:, head_idx].add(diff).at[:, tail_idx].add(-diff), None)
        acc, _ = lax.scan(step, jnp.zeros((K, VERTS), jnp.float32), (first_b, second_b, weight_b))
        return acc + ground[None, :] * field
    solution = jnp.zeros_like(right)
    residual = right
    scaled_res = residual / diag[None, :]
    direction = scaled_res
    gamma = lax.optimization_barrier(jnp.sum(residual * scaled_res, axis=1))
    for step in range(ITERS):
        image = operate(direction)
        alpha = gamma / lax.optimization_barrier(jnp.sum(direction * image, axis=1))
        solution = solution + alpha[:, None] * direction
        residual = residual - alpha[:, None] * image
        scaled_res = residual / diag[None, :]
        following = lax.optimization_barrier(jnp.sum(residual * scaled_res, axis=1))
        direction = scaled_res + (following / gamma)[:, None] * direction
        gamma = following
    return (solution, residual)
```

```python
import functools

import jax
import jax.numpy as jnp
from jax import lax
from jax.experimental import pallas as pl
from jax.experimental.pallas import tpu as pltpu
from jax.sharding import PartitionSpec as P

MESH = pl.DeviceIdType.MESH
BF, F, I = jnp.bfloat16, jnp.float32, jnp.int32
NT = (((1,), (1,)), ((), ()))
K = 24
ITERS = 3
NX, NZ, NY = 4, 8, 4
OWN = 3
ROWS = 2 * OWN
LANES = 256
WIN, MID, SIDE = 32, 16, 8
EC = 4096


def split(value):
    high = value.astype(BF)
    return high, (value - high.astype(F)).astype(BF)


def onehot(index):
    lanes = lax.broadcasted_iota(I, (LANES, index.shape[1]), 0).astype(F).astype(BF)
    return jnp.where(lanes == index.astype(F).astype(BF), jnp.ones((), BF), jnp.zeros((), BF))


def edge_rows(eb, c):
    block, row = c // 2, c % 2
    heads = eb[block, pl.ds(row, 1), :].astype(I)
    tails = eb[block, pl.ds(2 + row, 1), :].astype(I)
    weight = eb[block, pl.ds(4 + row, 1), :]
    return block, row, heads, tails, weight


def masks(heads, tails):
    ec = heads.shape[1]
    at_tail = lax.broadcasted_iota(I, (WIN, ec), 0) == (tails >> 8)
    at_head = lax.broadcasted_iota(I, (MID, ec), 0) == (heads >> 8)
    return at_tail, at_head


def spread(mask, parts):
    ones = jnp.where(mask, 1.0, 0.0).astype(BF)
    return jnp.concatenate([ones * parts[k][q] for q in range(2) for k in range(len(parts))], axis=0)


def sketch_edges(eb, shift, total_t, total_h, acc):
    rows = ROWS + 1
    nt, nh = rows * WIN, rows * MID
    total_t[...] = jnp.zeros_like(total_t)
    total_h[...] = jnp.zeros_like(total_h)

    def body(c, carry):
        block, row, heads, tails, weight = edge_rows(eb, c)
        bits = eb[block, pl.ds(6 + row, 1), :].astype(I) >> shift
        at_tail, at_head = masks(heads, tails)
        root = jnp.sqrt(weight)
        high, low = split(root)
        high, low = high.astype(F), low.astype(F)
        parts = []
        for k in range(ROWS):
            positive = ((bits >> k) & 1) == 1
            parts.append(
                (jnp.where(positive, high, -high).astype(BF), jnp.where(positive, low, -low).astype(BF))
            )
        w_high, w_low = split(weight)
        total_t[...] += lax.dot_general(
            spread(at_tail, parts + [(-w_high, -w_low)]), onehot(tails & 255), NT, preferred_element_type=F
        )
        total_h[...] += lax.dot_general(
            spread(at_head, parts + [(w_high, w_low)]), onehot(heads & 255), NT, preferred_element_type=F
        )
        return carry

    lax.fori_loop(0, 2 * NY, body, 0)
    both = -(total_t[:nt] + total_t[nt:]).reshape(rows, WIN, LANES)
    middle = (total_h[:nh] + total_h[nh:]).reshape(rows, MID, LANES)
    for core in range(2):
        for k in range(OWN + 1):
            source = OWN * core + k if k < OWN else ROWS
            acc[core, k] = both[source]
            acc[core, k, SIDE : SIDE + MID] += middle[source]


def apply_edges(eb, table, tab_t, tab_h, total_t, total_h, acc):
    nt, nh = ROWS * WIN, ROWS * MID
    for core in range(2):
        high, low = split(table[core])
        at, ah = OWN * core * WIN, OWN * core * MID
        tab_t[at : at + OWN * WIN] = high.reshape(OWN * WIN, LANES)
        tab_t[nt + at : nt + at + OWN * WIN] = low.reshape(OWN * WIN, LANES)
        tab_h[ah : ah + OWN * MID] = high[:, SIDE : SIDE + MID].reshape(OWN * MID, LANES)
        tab_h[nh + ah : nh + ah + OWN * MID] = low[:, SIDE : SIDE + MID].reshape(OWN * MID, LANES)
    total_t[...] = jnp.zeros_like(total_t)
    total_h[...] = jnp.zeros_like(total_h)

    def body(c, carry):
        _, _, heads, tails, weight = edge_rows(eb, c)
        at_tail, at_head = masks(heads, tails)
        hot_t, hot_h = onehot(tails & 255), onehot(heads & 255)
        from_t = jnp.dot(tab_t[...], hot_t, preferred_element_type=F)
        from_h = jnp.dot(tab_h[...], hot_h, preferred_element_type=F)
        parts = []
        for k in range(ROWS):
            t_rows = from_t[WIN * k : WIN * (k + 1)] + from_t[nt + WIN * k : nt + WIN * (k + 1)]
            h_rows = from_h[MID * k : MID * (k + 1)] + from_h[nh + MID * k : nh + MID * (k + 1)]
            t_sum = jnp.where(at_tail, t_rows, 0.0).reshape(WIN // 8, 8, EC).sum(0)
            h_sum = jnp.where(at_head, h_rows, 0.0).reshape(MID // 8, 8, EC).sum(0)
            parts.append(split(weight * jnp.sum(h_sum - t_sum, axis=0, keepdims=True)))
        total_t[: 2 * nt] += lax.dot_general(spread(at_tail, parts), hot_t, NT, preferred_element_type=F)
        total_h[: 2 * nh] += lax.dot_general(spread(at_head, parts), hot_h, NT, preferred_element_type=F)
        return carry

    lax.fori_loop(0, 2 * NY, body, 0)
    both = -(total_t[:nt] + total_t[nt : 2 * nt]).reshape(ROWS, WIN, LANES)
    middle = (total_h[:nh] + total_h[nh : 2 * nh]).reshape(ROWS, MID, LANES)
    for core in range(2):
        for k in range(OWN):
            acc[core, k] = both[OWN * core + k]
            acc[core, k, SIDE : SIDE + MID] += middle[OWN * core + k]


def kernel(
    edges, ground, sol, res,
    eb, gb, table, acc, in_mid, in_left, in_right,
    tab_t, tab_h, total_t, total_h, state, stat_x, stat_z, out_s, out_r,
    ag_s, ag_r, gr_s, gr_r, a_s, a_r, b_s, b_r, x_s, x_r, z_s, z_r, o_s, o_r,
):
    dom, grp = lax.axis_index("dom"), lax.axis_index("grp")
    z, x = dom // NX, dom % NX
    y, core = grp // 2, grp % 2
    other = 1 - core
    left, right = (dom + NX * NZ - 1) % (NX * NZ), (dom + 1) % (NX * NZ)
    near = [(dom, 2 * y + other)]
    near += [(left, 2 * y + (core + rc) % 2) for rc in range(2)]
    near += [(right, 2 * y + (core + rc) % 2) for rc in range(2)]
    group = [(dom, (grp + j) % 8) for j in range(1, 8)]
    along_x = [(z * NX + (x + j) % NX, grp) for j in range(1, NX)]
    along_z = [(((z + j) % NZ) * NX + x, grp) for j in range(1, NZ)]

    stat_x[...] = jnp.zeros_like(stat_x)
    barrier = pltpu.get_barrier_semaphore()
    peers = group + near[1:] + along_x + along_z
    for peer in peers:
        pl.semaphore_signal(barrier, inc=1, device_id=peer, device_id_type=MESH)
    pl.semaphore_wait(barrier, len(peers))

    def send(source, target, sems, at, peer):
        copy = pltpu.make_async_remote_copy(
            src_ref=source, dst_ref=target, send_sem=sems[0].at[at], recv_sem=sems[1].at[at],
            device_id=peer, device_id_type=MESH,
        )
        copy.start()
        return copy

    def finish(copies):
        for copy in copies:
            copy.wait()

    copies = []
    for j in range(1, NY):
        to = (y + j) % NY
        copies.append(send(edges.at[to // 2], eb.at[y], (ag_s, ag_r), j - 1, (dom, 2 * to + core)))
    for j in range(1, 8):
        copies.append(send(ground, gb.at[grp], (gr_s, gr_r), j - 1, group[j - 1]))
    eb[y] = edges[y // 2]
    gb[grp] = ground[...]
    finish(copies)

    def fold(rows):
        sems = (b_s, b_r)
        copies = [send(acc.at[other, :rows, SIDE : SIDE + MID], in_mid.at[:rows], sems, 0, near[0])]
        for rc in range(2):
            theirs = (core + rc) % 2
            copies.append(send(acc.at[theirs, :rows, :SIDE], in_right.at[rc, :rows], sems, 1 + rc, near[1 + rc]))
            copies.append(
                send(acc.at[theirs, :rows, SIDE + MID :], in_left.at[rc, :rows], sems, 3 + rc, near[3 + rc])
            )
        finish(copies)
        sums = []
        for k in range(rows):
            low = in_left[0, k] + in_left[1, k]
            high = in_right[0, k] + in_right[1, k]
            sums.append(acc[core, k, SIDE : SIDE + MID] + in_mid[k] + jnp.concatenate([low, high], axis=0))
        return sums

    def share():
        sems = (a_s, a_r)
        mine = table.at[core]
        copies = [send(mine.at[:, SIDE : SIDE + MID], mine.at[:, SIDE : SIDE + MID], sems, 0, near[0])]
        for rc in range(2):
            copies.append(send(mine.at[:, SIDE : 2 * SIDE], mine.at[:, SIDE + MID :], sems, 1 + rc, near[1 + rc]))
            copies.append(send(mine.at[:, MID : SIDE + MID], mine.at[:, :SIDE], sems, 3 + rc, near[3 + rc]))
        finish(copies)

    def reduce_all(it, values):
        for row, value in enumerate(values):
            lanes = jnp.sum(value, axis=0, keepdims=True)
            stat_x[it, x, row : row + 1, :] = lanes[:, :128] + lanes[:, 128:]
        copies = []
        for j in range(1, NX):
            here = stat_x.at[it, x]
            copies.append(send(here, here, (x_s.at[it], x_r.at[it]), j - 1, along_x[j - 1]))
        finish(copies)
        stat_z[it, z] = (stat_x[it, 0] + stat_x[it, 1]) + (stat_x[it, 2] + stat_x[it, 3])
        copies = []
        for j in range(1, NZ):
            here = stat_z.at[it, z]
            copies.append(send(here, here, (z_s.at[it], z_r.at[it]), j - 1, along_z[j - 1]))
        finish(copies)
        whole = stat_z[it, 0]
        for j in range(1, NZ):
            whole = whole + stat_z[it, j]
        return jnp.sum(whole, axis=1, keepdims=True)

    DIAG, GROUND, R, PP, S, X = 0, 1, 2, 2 + OWN, 2 + 2 * OWN, 2 + 3 * OWN
    for j in range(8):
        state[GROUND, 2 * j : 2 * j + 2, :] = gb[j]
    sketch_edges(eb, 6 * (y % 2), total_t, total_h, acc)
    sums = fold(OWN + 1)
    state[DIAG] = sums[OWN] + state[GROUND]
    for k in range(OWN):
        state[R + k] = sums[k]
        table[core, k, SIDE : SIDE + MID] = sums[k] / state[DIAG]

    gamma_was = curve_was = None
    for it in range(ITERS):
        share()
        apply_edges(eb, table, tab_t, tab_h, total_t, total_h, acc)
        sums = fold(OWN)
        u = [table[core, k, SIDE : SIDE + MID] for k in range(OWN)]
        image = [sums[k] + state[GROUND] * u[k] for k in range(OWN)]
        values = [state[R + k] * u[k] for k in range(OWN)] + [u[k] * image[k] for k in range(OWN)]
        if it:
            values += [u[k] * state[S + k] for k in range(OWN)]
        totals = reduce_all(it, values)
        gamma, curve = totals[:OWN], totals[OWN : 2 * OWN]
        if it:
            beta = gamma / gamma_was
            curve = curve + 2.0 * beta * totals[2 * OWN : 3 * OWN] + beta * beta * curve_was
        alpha = gamma / curve
        for k in range(OWN):
            a = alpha[k : k + 1]
            if it:
                b = beta[k : k + 1]
                direction = u[k] + b * state[PP + k]
                along = image[k] + b * state[S + k]
                state[X + k] = state[X + k] + a * direction
            else:
                direction, along = u[k], image[k]
                state[X + k] = a * direction
            state[PP + k] = direction
            state[S + k] = along
            rest = state[R + k] - a * along
            state[R + k] = rest
            if it < ITERS - 1:
                table[core, k, SIDE : SIDE + MID] = rest / state[DIAG]
        gamma_was, curve_was = gamma, curve

    for g in range(8):
        for k in range(OWN):
            for half in range(2):
                lanes = slice(LANES * half, LANES * (half + 1))
                tile = slice(2 * g + half, 2 * g + half + 1)
                out_s[g, k : k + 1, lanes] = state[X + k, tile, :]
                out_s[g, OWN + k : OWN + k + 1, lanes] = state[R + k, tile, :]
    copies = []
    for j in range(1, 8):
        to = (grp + j) % 8
        copies.append(send(out_s.at[to], out_r.at[grp], (o_s, o_r), j - 1, group[j - 1]))
    out_r[grp] = out_s[grp]
    finish(copies)
    for g in range(8):
        sol[OWN * g : OWN * (g + 1), :] = out_r[g, :OWN, :]
        res[OWN * g : OWN * (g + 1), :] = out_r[g, OWN : 2 * OWN, :]


def on_device(heads, tails, signs, edge_weights, ground):
    common = [heads.astype(F).reshape(2, EC), tails.astype(F).reshape(2, EC), edge_weights.reshape(2, EC)]
    words = signs.astype(F).reshape(2, 2, EC)
    edges = jnp.stack([jnp.concatenate(common + [words[j]], axis=0) for j in range(2)])
    dma = lambda *shape: pltpu.SemaphoreType.DMA(shape)
    vmem = pl.BlockSpec(memory_space=pltpu.VMEM)
    out = jax.ShapeDtypeStruct((K, 512), F)
    scratch = [
        pltpu.VMEM((NY, 8, EC), F),
        pltpu.VMEM((8, 2, LANES), F),
        pltpu.VMEM((2, OWN, WIN, LANES), F),
        pltpu.VMEM((2, OWN + 1, WIN, LANES), F),
        pltpu.VMEM((OWN + 1, MID, LANES), F),
        pltpu.VMEM((2, OWN + 1, SIDE, LANES), F),
        pltpu.VMEM((2, OWN + 1, SIDE, LANES), F),
        pltpu.VMEM((2 * ROWS * WIN, LANES), BF),
        pltpu.VMEM((2 * ROWS * MID, LANES), BF),
        pltpu.VMEM((2 * (ROWS + 1) * WIN, LANES), F),
        pltpu.VMEM((2 * (ROWS + 1) * MID, LANES), F),
        pltpu.VMEM((2 + 4 * OWN, MID, LANES), F),
        pltpu.VMEM((ITERS, NX, 16, 128), F),
        pltpu.VMEM((ITERS, NZ, 16, 128), F),
        pltpu.VMEM((8, 8, 512), F),
        pltpu.VMEM((8, 8, 512), F),
    ]
    counts = [(NY - 1,), (7,), (5,), (5,), (ITERS, NX - 1), (ITERS, NZ - 1), (7,)]
    scratch += [dma(*count) for count in counts for _ in range(2)]
    return pl.pallas_call(
        kernel,
        out_shape=(out, out),
        in_specs=[vmem, vmem],
        out_specs=(vmem, vmem),
        scratch_shapes=scratch,
        compiler_params=pltpu.CompilerParams(
            collective_id=0, has_side_effects=True, vmem_limit_bytes=56 * 2**20
        ),
        name="resistances",
    )(edges, ground.reshape(2, LANES))


def solution(mesh):
    in_specs = (
        P(("dom", "grp")),
        P(("dom", "grp")),
        P(None, ("dom", "grp")),
        P(("dom", "grp")),
        P(("dom", "grp")),
    )
    out_specs = (P(None, ("dom", "grp")), P(None, ("dom", "grp")))
    return jax.shard_map(
        on_device, mesh=mesh, in_specs=in_specs, out_specs=out_specs, check_vma=False
    )
```

```python
import functools

import jax
import jax.numpy as jnp
from jax import lax
from jax.experimental import pallas as pl
from jax.experimental.pallas import tpu as pltpu
from jax.sharding import PartitionSpec as P

MESH = pl.DeviceIdType.MESH
BF, F, I = jnp.bfloat16, jnp.float32, jnp.int32
NT = (((1,), (1,)), ((), ()))
K = 24
ITERS = 3
NX, NZ, NY = 4, 8, 4
OWN = 3
ROWS = 2 * OWN
LANES = 256
WIN, MID, SIDE = 32, 16, 8
EC = 4096
WIDE = 1024
COL_H, TILE_H, COL_T, TILE_T, WEIGHT, SIGNS = range(6)


def split(value):
    high = value.astype(BF)
    return high, (value - high.astype(F)).astype(BF)


def onehot(index):
    lanes = lax.broadcasted_iota(I, (LANES, index.shape[1]), 0).astype(F).astype(BF)
    return jnp.where(lanes == index.astype(BF), jnp.ones((), BF), jnp.zeros((), BF))


def edge_row(pre, c, name):
    block, first = c // 2, (c % 2) * (EC // WIDE)
    return jnp.concatenate([pre[block, name, pl.ds(first + q, 1), :] for q in range(EC // WIDE)], axis=1)


def at_tile(row, tiles):
    return lax.broadcasted_iota(I, (tiles, row.shape[1]), 0).astype(F) == row


def spread(mask, parts):
    ones = jnp.where(mask, 1.0, 0.0).astype(BF)
    return jnp.concatenate([ones * parts[k][q] for q in range(2) for k in range(len(parts))], axis=0)


def prepare(eb, pre, block):
    for source, col, tile in ((0, COL_H, TILE_H), (1, COL_T, TILE_T)):
        whole = eb[block, source].astype(I)
        pre[block, col] = (whole & (LANES - 1)).astype(F)
        pre[block, tile] = (whole >> 8).astype(F)
    pre[block, WEIGHT] = eb[block, 2]
    pre[block, SIGNS] = eb[block, 3]


def sketch_tails(pre, c, shift, diffs, total_t):
    weight = edge_row(pre, c, WEIGHT)
    bits = edge_row(pre, c, SIGNS).astype(I) >> shift
    root = jnp.sqrt(weight)
    parts = []
    for k in range(ROWS):
        value = jnp.where(((bits >> k) & 1) == 1, root, -root)
        diffs[c, k : k + 1, :] = value
        parts.append(split(value))
    diffs[c, ROWS : ROWS + 1, :] = weight
    parts.append(split(-weight))
    hot = onehot(edge_row(pre, c, COL_T))
    total_t[...] += lax.dot_general(
        spread(at_tile(edge_row(pre, c, TILE_T), WIN), parts), hot, NT, preferred_element_type=F
    )


def gather_heads(pre, c, tab_h, first_values):
    nh = ROWS * MID
    got = jnp.dot(tab_h[...], onehot(edge_row(pre, c, COL_H)), preferred_element_type=F)
    mask = at_tile(edge_row(pre, c, TILE_H), MID)
    for k in range(ROWS):
        rows = got[MID * k : MID * (k + 1)] + got[nh + MID * k : nh + MID * (k + 1)]
        first_values[c, k] = jnp.where(mask, rows, 0.0).reshape(MID // 8, 8, EC).sum(0)


def apply_tails(pre, c, tab_t, first_values, diffs, energy, total_t):
    nt = ROWS * WIN
    hot = onehot(edge_row(pre, c, COL_T))
    mask = at_tile(edge_row(pre, c, TILE_T), WIN)
    weight = edge_row(pre, c, WEIGHT)
    got = jnp.dot(tab_t[...], hot, preferred_element_type=F)
    parts = []
    for k in range(ROWS):
        rows = got[WIN * k : WIN * (k + 1)] + got[nt + WIN * k : nt + WIN * (k + 1)]
        second = jnp.where(mask, rows, 0.0).reshape(WIN // 8, 8, EC).sum(0)
        gap = jnp.sum(first_values[c, k] - second, axis=0, keepdims=True)
        diff = weight * gap
        diffs[c, k : k + 1, :] = diff
        work = diff * gap
        energy[k : k + 1, :] += sum(work[:, 128 * j : 128 * (j + 1)] for j in range(EC // 128))
        parts.append(split(diff))
    total_t[: 2 * nt] += lax.dot_general(spread(mask, parts), hot, NT, preferred_element_type=F)


def scatter_heads(pre, c, rows, diffs, total_h):
    parts = [split(diffs[c, k : k + 1, :]) for k in range(rows)]
    total_h[: 2 * rows * MID] += lax.dot_general(
        spread(at_tile(edge_row(pre, c, TILE_H), MID), parts),
        onehot(edge_row(pre, c, COL_H)), NT, preferred_element_type=F,
    )


def tables(table, core, tab, first, tiles):
    n, at = ROWS * tiles, OWN * tiles * core
    high, low = split(table[core, :, first : first + tiles])
    tab[at : at + OWN * tiles] = high.reshape(OWN * tiles, LANES)
    tab[n + at : n + at + OWN * tiles] = low.reshape(OWN * tiles, LANES)


def kernel(
    heads, tails, weights, signs, ground, sol, res,
    eb_s, eb, pre, gb, table, acc, in_mid, in_left, in_right, first_values, diffs, energy,
    tab_t, tab_h, total_t, total_h, state, stat_s, stat_x, stat_z, out_s, out_r,
    ag_s, ag_r, gr_s, gr_r, a_s, a_r, b_s, b_r, x_s, x_r, z_s, z_r, o_s, o_r,
):
    dom, grp = lax.axis_index("dom"), lax.axis_index("grp")
    z, x = dom // NX, dom % NX
    y, core = grp // 2, grp % 2
    other = 1 - core
    left, right = (dom + NX * NZ - 1) % (NX * NZ), (dom + 1) % (NX * NZ)
    near = [(dom, 2 * y + other)]
    near += [(left, 2 * y + (core + rc) % 2) for rc in range(2)]
    near += [(right, 2 * y + (core + rc) % 2) for rc in range(2)]
    group = [(dom, (grp + j) % 8) for j in range(1, 8)]
    along_x = [(z * NX + (x + j) % NX, 2 * y + (core + rc) % 2) for j in range(NX) for rc in range(2)]
    along_z = [(((z + j) % NZ) * NX + x, grp) for j in range(1, NZ)]

    barrier = pltpu.get_barrier_semaphore()
    peers = group + near[1:] + along_x[2:] + along_z
    for peer in peers:
        pl.semaphore_signal(barrier, inc=1, device_id=peer, device_id_type=MESH)

    for word in range(2):
        for j in range(8):
            lanes = slice(128 * j, 128 * (j + 1))
            rows = slice(8 * j, 8 * (j + 1))
            eb_s[word, 0, :, lanes] = heads[rows, :].astype(F)
            eb_s[word, 1, :, lanes] = tails[rows, :].astype(F)
            eb_s[word, 2, :, lanes] = weights[rows, :]
        for row in range(8):
            pieces = [signs[word : word + 1, 128 * (8 * j + row) : 128 * (8 * j + row + 1)] for j in range(8)]
            eb_s[word, 3, row : row + 1, :] = jnp.concatenate(pieces, axis=1).astype(F)
    pl.semaphore_wait(barrier, len(peers))

    def send(source, target, sems, at, peer):
        copy = pltpu.make_async_remote_copy(
            src_ref=source, dst_ref=target, send_sem=sems[0].at[at], recv_sem=sems[1].at[at],
            device_id=peer, device_id_type=MESH,
        )
        copy.start()
        return copy

    def finish(copies):
        for copy in copies:
            copy.wait()

    arriving = []
    for j in range(1, NY):
        to = (y + j) % NY
        arriving.append(send(eb_s.at[to // 2], eb.at[y], (ag_s, ag_r), j - 1, (dom, 2 * to + core)))
    grounds = [send(ground, gb.at[grp], (gr_s, gr_r), j - 1, group[j - 1]) for j in range(1, 8)]
    eb[y] = eb_s[y // 2]
    gb[grp] = ground[...]

    def send_borders(rows):
        copies = []
        for rc in range(2):
            theirs = (core + rc) % 2
            copies.append(
                send(acc.at[theirs, :rows, :SIDE], in_right.at[rc, :rows], (b_s, b_r), 1 + rc, near[1 + rc])
            )
            copies.append(
                send(acc.at[theirs, :rows, SIDE + MID :], in_left.at[rc, :rows], (b_s, b_r), 3 + rc, near[3 + rc])
            )
        return copies

    def send_middle(rows):
        return send(acc.at[other, :rows, SIDE : SIDE + MID], in_mid.at[:rows], (b_s, b_r), 0, near[0])

    def folded(k):
        low = in_left[0, k] + in_left[1, k]
        high = in_right[0, k] + in_right[1, k]
        return acc[core, k, SIDE : SIDE + MID] + in_mid[k] + jnp.concatenate([low, high], axis=0)

    def keep_tails(rows):
        n = rows * WIN
        for c in range(2):
            for k in range(OWN + (rows > ROWS)):
                at = WIN * (OWN * c + k if k < OWN else ROWS)
                whole = total_t[at : at + WIN] + total_t[n + at : n + at + WIN]
                acc[c, k] = -whole

    def keep_heads(rows):
        n = rows * MID
        for c in range(2):
            for k in range(OWN + (rows > ROWS)):
                at = MID * (OWN * c + k if k < OWN else ROWS)
                acc[c, k, SIDE : SIDE + MID] += total_h[at : at + MID] + total_h[n + at : n + at + MID]

    def loop(first, last, step):
        def body(c, carry):
            step(c)
            return carry

        lax.fori_loop(first, last, body, 0)

    def lanes_of(value):
        row = jnp.sum(value, axis=0, keepdims=True)
        return row[:, :128] + row[:, 128:]

    DIAG, GROUND, R, PP, S, X = 0, 1, 2, 2 + OWN, 2 + 2 * OWN, 2 + 3 * OWN
    CHUNKS = 2 * NY
    shift = ROWS * (y % 2)

    total_t[...] = jnp.zeros_like(total_t)
    total_h[...] = jnp.zeros_like(total_h)
    for j in range(NY):
        block = (y + NY - j) % NY
        if j:
            arriving[j - 1].wait()
        prepare(eb, pre, block)
        loop(0, 2, lambda half: sketch_tails(pre, 2 * block + half, shift, diffs, total_t))
    keep_tails(ROWS + 1)
    borders = send_borders(OWN + 1)
    loop(0, CHUNKS, lambda c: scatter_heads(pre, c, ROWS + 1, diffs, total_h))
    keep_heads(ROWS + 1)
    middle = send_middle(OWN + 1)
    finish(grounds)
    for j in range(8):
        for row in range(4):
            lanes = slice(128 * (row % 2), 128 * (row % 2 + 1))
            state[GROUND, 2 * j + row // 2 : 2 * j + row // 2 + 1, lanes] = gb[j, row : row + 1, :]
    finish(borders + [middle])
    state[DIAG] = folded(OWN) + state[GROUND]
    for k in range(OWN):
        state[R + k] = folded(k)
        table[core, k, SIDE : SIDE + MID] = state[R + k] / state[DIAG]

    gamma_was = curve_was = None
    for it in range(ITERS):
        mine = table.at[core]
        to_partner = send(mine.at[:, SIDE : SIDE + MID], mine.at[:, SIDE : SIDE + MID], (a_s, a_r), 0, near[0])
        halos = []
        for rc in range(2):
            halos.append(send(mine.at[:, SIDE : 2 * SIDE], mine.at[:, SIDE + MID :], (a_s, a_r), 1 + rc, near[1 + rc]))
            halos.append(send(mine.at[:, MID : SIDE + MID], mine.at[:, :SIDE], (a_s, a_r), 3 + rc, near[3 + rc]))
        total_t[...] = jnp.zeros_like(total_t)
        total_h[...] = jnp.zeros_like(total_h)
        energy[...] = jnp.zeros_like(energy)
        stat_s[it] = jnp.zeros_like(stat_s[it])
        for k in range(OWN):
            u = table[core, k, SIDE : SIDE + MID]
            stat_s[it, core, OWN + k : OWN + k + 1, :] = lanes_of(state[R + k] * u)
            if it:
                stat_s[it, core, 2 * OWN + k : 2 * OWN + k + 1, :] = lanes_of(state[S + k] * u)
        to_partner.wait()
        for c in range(2):
            tables(table, c, tab_h, SIDE, MID)
        loop(0, CHUNKS, lambda c: gather_heads(pre, c, tab_h, first_values))
        finish(halos)
        for c in range(2):
            tables(table, c, tab_t, 0, WIN)
        loop(0, CHUNKS, lambda c: apply_tails(pre, c, tab_t, first_values, diffs, energy, total_t))
        keep_tails(ROWS)
        borders = send_borders(OWN)

        for c in range(2):
            stat_s[it, c, :OWN, :] = energy[OWN * c : OWN * (c + 1), :]
        for k in range(OWN):
            u = table[core, k, SIDE : SIDE + MID]
            stat_s[it, core, k : k + 1, :] += lanes_of(state[GROUND] * u * u)
        slot = 2 * x + core
        copies = []
        for at in range(1, 2 * NX):
            theirs = (core + at % 2) % 2
            copies.append(
                send(stat_s.at[it, theirs], stat_x.at[it, slot], (x_s.at[it], x_r.at[it]), at - 1, along_x[at])
            )
        stat_x[it, slot] = stat_s[it, core]
        loop(0, CHUNKS // 2, lambda c: scatter_heads(pre, c, ROWS, diffs, total_h))
        finish(copies)
        part = stat_x[it, 0]
        for j in range(1, 2 * NX):
            part = part + stat_x[it, j]
        stat_z[it, z] = part
        copies = []
        for j in range(1, NZ):
            here = stat_z.at[it, z]
            copies.append(send(here, here, (z_s.at[it], z_r.at[it]), j - 1, along_z[j - 1]))
        loop(CHUNKS // 2, CHUNKS, lambda c: scatter_heads(pre, c, ROWS, diffs, total_h))
        keep_heads(ROWS)
        middle = send_middle(OWN)
        finish(copies)
        whole = stat_z[it, 0]
        for j in range(1, NZ):
            whole = whole + stat_z[it, j]
        totals = jnp.sum(whole, axis=1, keepdims=True)
        curve, gamma = totals[:OWN], totals[OWN : 2 * OWN]
        if it:
            beta = gamma / gamma_was
            curve = curve + 2.0 * beta * totals[2 * OWN : 3 * OWN] + beta * beta * curve_was
        alpha = gamma / curve
        finish(borders + [middle])
        for k in range(OWN):
            a = alpha[k : k + 1]
            u = table[core, k, SIDE : SIDE + MID]
            image = folded(k) + state[GROUND] * u
            if it:
                b = beta[k : k + 1]
                direction = u + b * state[PP + k]
                along = image + b * state[S + k]
                state[X + k] = state[X + k] + a * direction
            else:
                direction, along = u, image
                state[X + k] = a * direction
            state[PP + k] = direction
            state[S + k] = along
            rest = state[R + k] - a * along
            state[R + k] = rest
            if it < ITERS - 1:
                table[core, k, SIDE : SIDE + MID] = rest / state[DIAG]
        gamma_was, curve_was = gamma, curve

    for g in range(8):
        for k in range(OWN):
            for half in range(2):
                lanes = slice(LANES * half, LANES * (half + 1))
                tile = slice(2 * g + half, 2 * g + half + 1)
                out_s[g, k : k + 1, lanes] = state[X + k, tile, :]
                out_s[g, OWN + k : OWN + k + 1, lanes] = state[R + k, tile, :]
    copies = []
    for j in range(1, 8):
        to = (grp + j) % 8
        copies.append(send(out_s.at[to], out_r.at[grp], (o_s, o_r), j - 1, group[j - 1]))
    out_r[grp] = out_s[grp]
    finish(copies)
    for g in range(8):
        sol[OWN * g : OWN * (g + 1), :] = out_r[g, :OWN, :]
        res[OWN * g : OWN * (g + 1), :] = out_r[g, OWN : 2 * OWN, :]


def on_device(heads, tails, signs, edge_weights, ground):
    dma = lambda *shape: pltpu.SemaphoreType.DMA(shape)
    vmem = pl.BlockSpec(memory_space=pltpu.VMEM)
    out = jax.ShapeDtypeStruct((K, 512), F)
    scratch = [
        pltpu.VMEM((2, 4, 8, WIDE), F),
        pltpu.VMEM((NY, 4, 8, WIDE), F),
        pltpu.VMEM((NY, 6, 8, WIDE), F),
        pltpu.VMEM((8, 4, 128), F),
        pltpu.VMEM((2, OWN, WIN, LANES), F),
        pltpu.VMEM((2, OWN + 1, WIN, LANES), F),
        pltpu.VMEM((OWN + 1, MID, LANES), F),
        pltpu.VMEM((2, OWN + 1, SIDE, LANES), F),
        pltpu.VMEM((2, OWN + 1, SIDE, LANES), F),
        pltpu.VMEM((2 * NY, ROWS, 8, EC), F),
        pltpu.VMEM((2 * NY, 8, EC), F),
        pltpu.VMEM((8, 128), F),
        pltpu.VMEM((2 * ROWS * WIN, LANES), BF),
        pltpu.VMEM((2 * ROWS * MID, LANES), BF),
        pltpu.VMEM((2 * (ROWS + 1) * WIN, LANES), F),
        pltpu.VMEM((2 * (ROWS + 1) * MID, LANES), F),
        pltpu.VMEM((2 + 4 * OWN, MID, LANES), F),
        pltpu.VMEM((ITERS, 2, 16, 128), F),
        pltpu.VMEM((ITERS, 2 * NX, 16, 128), F),
        pltpu.VMEM((ITERS, NZ, 16, 128), F),
        pltpu.VMEM((8, 8, 512), F),
        pltpu.VMEM((8, 8, 512), F),
    ]
    counts = [(NY - 1,), (7,), (5,), (5,), (ITERS, 2 * NX - 1), (ITERS, NZ - 1), (7,)]
    scratch += [dma(*count) for count in counts for _ in range(2)]
    return pl.pallas_call(
        kernel,
        out_shape=(out, out),
        in_specs=[vmem] * 5,
        out_specs=(vmem, vmem),
        scratch_shapes=scratch,
        compiler_params=pltpu.CompilerParams(
            collective_id=0, has_side_effects=True, vmem_limit_bytes=58 * 2**20
        ),
        name="resistances",
    )(
        heads.reshape(64, 128), tails.reshape(64, 128), edge_weights.reshape(64, 128), signs, ground.reshape(4, 128)
    )


def solution(mesh):
    in_specs = (
        P(("dom", "grp")),
        P(("dom", "grp")),
        P(None, ("dom", "grp")),
        P(("dom", "grp")),
        P(("dom", "grp")),
    )
    out_specs = (P(None, ("dom", "grp")), P(None, ("dom", "grp")))
    return jax.shard_map(
        on_device, mesh=mesh, in_specs=in_specs, out_specs=out_specs, check_vma=False
    )
```

```python
import functools

import jax
import jax.numpy as jnp
from jax import lax
from jax.experimental import pallas as pl
from jax.experimental.pallas import tpu as pltpu
from jax.sharding import PartitionSpec as P

MESH = pl.DeviceIdType.MESH
BF, F, I = jnp.bfloat16, jnp.float32, jnp.int32
NT = (((1,), (1,)), ((), ()))
K = 24
ITERS = 3
NX, NZ, NY = 4, 8, 4
OWN = 3
ROWS = 2 * OWN
LANES = 256
WIN, MID, SIDE = 32, 16, 8
EC = 8192
WIDE = 1024
COL_H, TILE_H, COL_T, TILE_T, WEIGHT, SIGNS = range(6)


def split(value):
    high = value.astype(BF)
    return high, (value - high.astype(F)).astype(BF)


def onehot(index):
    lanes = lax.broadcasted_iota(I, (LANES, index.shape[1]), 0).astype(F).astype(BF)
    return jnp.where(lanes == index.astype(BF), jnp.ones((), BF), jnp.zeros((), BF))


def edge_row(pre, c, name):
    return jnp.concatenate([pre[c, name, q : q + 1, :] for q in range(EC // WIDE)], axis=1)


def at_tile(row, tiles):
    return lax.broadcasted_iota(I, (tiles, row.shape[1]), 0).astype(F) == row


def spread(mask, parts):
    ones = jnp.where(mask, 1.0, 0.0).astype(BF)
    return jnp.concatenate([ones * parts[k][q] for q in range(2) for k in range(len(parts))], axis=0)


def prepare(eb, pre, block):
    for source, col, tile in ((0, COL_H, TILE_H), (1, COL_T, TILE_T)):
        whole = eb[block, source].astype(I)
        pre[block, col] = (whole & (LANES - 1)).astype(F)
        pre[block, tile] = (whole >> 8).astype(F)
    pre[block, WEIGHT] = eb[block, 2]
    pre[block, SIGNS] = eb[block, 3]


def sketch_values(pre, c, shift, diffs):
    weight = edge_row(pre, c, WEIGHT)
    bits = edge_row(pre, c, SIGNS).astype(I) >> shift
    root = jnp.sqrt(weight)
    for k in range(ROWS):
        diffs[c, k : k + 1, :] = jnp.where(((bits >> k) & 1) == 1, root, -root)
    diffs[c, ROWS : ROWS + 1, :] = weight


def gather_heads(pre, c, tab_h, first_values):
    nh = ROWS * MID
    got = jnp.dot(tab_h[...], onehot(edge_row(pre, c, COL_H)), preferred_element_type=F)
    mask = at_tile(edge_row(pre, c, TILE_H), MID)
    for k in range(ROWS):
        rows = got[MID * k : MID * (k + 1)] + got[nh + MID * k : nh + MID * (k + 1)]
        first_values[c, k] = jnp.where(mask, rows, 0.0).reshape(MID // 8, 8, EC).sum(0)


def gather_tails(pre, c, tab_t, first_values, diffs, energy):
    nt = ROWS * WIN
    got = jnp.dot(tab_t[...], onehot(edge_row(pre, c, COL_T)), preferred_element_type=F)
    mask = at_tile(edge_row(pre, c, TILE_T), WIN)
    weight = edge_row(pre, c, WEIGHT)
    for k in range(ROWS):
        rows = got[WIN * k : WIN * (k + 1)] + got[nt + WIN * k : nt + WIN * (k + 1)]
        second = jnp.where(mask, rows, 0.0).reshape(WIN // 8, 8, EC).sum(0)
        gap = jnp.sum(first_values[c, k] - second, axis=0, keepdims=True)
        diff = weight * gap
        diffs[c, k : k + 1, :] = diff
        work = diff * gap
        energy[k : k + 1, :] += sum(work[:, 128 * j : 128 * (j + 1)] for j in range(EC // 128))


def scatter(pre, c, rows, tile, col, tiles, diffs, total):
    parts = [split(diffs[c, k : k + 1, :]) for k in range(rows)]
    total[: 2 * rows * tiles] += lax.dot_general(
        spread(at_tile(edge_row(pre, c, tile), tiles), parts),
        onehot(edge_row(pre, c, col)), NT, preferred_element_type=F,
    )


def tables(table, core, tab, first, tiles):
    n, at = ROWS * tiles, OWN * tiles * core
    high, low = split(table[core, :, first : first + tiles])
    tab[at : at + OWN * tiles] = high.reshape(OWN * tiles, LANES)
    tab[n + at : n + at + OWN * tiles] = low.reshape(OWN * tiles, LANES)


def kernel(
    heads, tails, weights, signs, ground, sol, res,
    eb_s, eb, pre, gb, table, acc, in_mid, in_left, in_right, first_values, diffs, energy,
    tab_t, tab_h, total_t, total_h, state, stat_s, stat_x, stat_z, out_s, out_r,
    ag_s, ag_r, gr_s, gr_r, a_s, a_r, b_s, b_r, x_s, x_r, z_s, z_r, o_s, o_r,
):
    dom, grp = lax.axis_index("dom"), lax.axis_index("grp")
    z, x = dom // NX, dom % NX
    y, core = grp // 2, grp % 2
    other = 1 - core
    left, right = (dom + NX * NZ - 1) % (NX * NZ), (dom + 1) % (NX * NZ)
    near = [(dom, 2 * y + other)]
    near += [(left, 2 * y + (core + rc) % 2) for rc in range(2)]
    near += [(right, 2 * y + (core + rc) % 2) for rc in range(2)]
    group = [(dom, (grp + j) % 8) for j in range(1, 8)]
    along_x = [(z * NX + (x + j) % NX, 2 * y + (core + rc) % 2) for j in range(NX) for rc in range(2)]
    along_z = [(((z + j) % NZ) * NX + x, grp) for j in range(1, NZ)]

    barrier = pltpu.get_barrier_semaphore()
    peers = group + near[1:] + along_x[2:] + along_z
    for peer in peers:
        pl.semaphore_signal(barrier, inc=1, device_id=peer, device_id_type=MESH)

    for word in range(2):
        for j in range(8):
            lanes = slice(128 * j, 128 * (j + 1))
            rows = slice(8 * j, 8 * (j + 1))
            eb_s[word, 0, :, lanes] = heads[rows, :].astype(F)
            eb_s[word, 1, :, lanes] = tails[rows, :].astype(F)
            eb_s[word, 2, :, lanes] = weights[rows, :]
        for row in range(8):
            pieces = [signs[word : word + 1, 128 * (8 * j + row) : 128 * (8 * j + row + 1)] for j in range(8)]
            eb_s[word, 3, row : row + 1, :] = jnp.concatenate(pieces, axis=1).astype(F)
    pl.semaphore_wait(barrier, len(peers))

    def send(source, target, sems, at, peer):
        copy = pltpu.make_async_remote_copy(
            src_ref=source, dst_ref=target, send_sem=sems[0].at[at], recv_sem=sems[1].at[at],
            device_id=peer, device_id_type=MESH,
        )
        copy.start()
        return copy

    def finish(copies):
        for copy in copies:
            copy.wait()

    arriving = []
    for j in range(1, NY):
        to = (y + j) % NY
        arriving.append(send(eb_s.at[to // 2], eb.at[y], (ag_s, ag_r), j - 1, (dom, 2 * to + core)))
    grounds = [send(ground, gb.at[grp], (gr_s, gr_r), j - 1, group[j - 1]) for j in range(1, 8)]
    eb[y] = eb_s[y // 2]
    gb[grp] = ground[...]

    def send_borders(rows):
        copies = []
        for rc in range(2):
            theirs = (core + rc) % 2
            copies.append(
                send(acc.at[theirs, :rows, :SIDE], in_right.at[rc, :rows], (b_s, b_r), 1 + rc, near[1 + rc])
            )
            copies.append(
                send(acc.at[theirs, :rows, SIDE + MID :], in_left.at[rc, :rows], (b_s, b_r), 3 + rc, near[3 + rc])
            )
        return copies

    def send_middle(rows):
        return send(acc.at[other, :rows, SIDE : SIDE + MID], in_mid.at[:rows], (b_s, b_r), 0, near[0])

    def folded(k):
        low = in_left[0, k] + in_left[1, k]
        high = in_right[0, k] + in_right[1, k]
        return acc[core, k, SIDE : SIDE + MID] + in_mid[k] + jnp.concatenate([low, high], axis=0)

    def keep_tails(rows):
        n = rows * WIN
        for c in range(2):
            for k in range(OWN + (rows > ROWS)):
                at = WIN * (OWN * c + k if k < OWN else ROWS)
                whole = total_t[at : at + WIN] + total_t[n + at : n + at + WIN]
                acc[c, k] = -whole if k < OWN else whole

    def keep_heads(rows):
        n = rows * MID
        for c in range(2):
            for k in range(OWN + (rows > ROWS)):
                at = MID * (OWN * c + k if k < OWN else ROWS)
                acc[c, k, SIDE : SIDE + MID] += total_h[at : at + MID] + total_h[n + at : n + at + MID]

    def loop(first, last, step):
        def body(c, carry):
            step(c)
            return carry

        lax.fori_loop(first, last, body, 0)

    def lanes_of(value):
        row = jnp.sum(value, axis=0, keepdims=True)
        return row[:, :128] + row[:, 128:]

    DIAG, GROUND, R, PP, S, X = 0, 1, 2, 2 + OWN, 2 + 2 * OWN, 2 + 3 * OWN
    shift = ROWS * (y % 2)

    total_t[...] = jnp.zeros_like(total_t)
    total_h[...] = jnp.zeros_like(total_h)
    def scatter_tails(c, rows):
        scatter(pre, c, rows, TILE_T, COL_T, WIN, diffs, total_t)

    def scatter_heads(c, rows):
        scatter(pre, c, rows, TILE_H, COL_H, MID, diffs, total_h)

    for j in (0, 1, 3, 2):
        block = (y + NY - j) % NY
        if j:
            arriving[j - 1].wait()
        prepare(eb, pre, block)
        sketch_values(pre, block, shift, diffs)
        scatter_tails(block, ROWS + 1)
        if not j:
            scatter_heads(block, ROWS + 1)
    keep_tails(ROWS + 1)
    borders = send_borders(OWN + 1)
    loop(1, NY, lambda j: scatter_heads((y + j) % NY, ROWS + 1))
    keep_heads(ROWS + 1)
    middle = send_middle(OWN + 1)
    finish(grounds)
    for j in range(8):
        for row in range(4):
            lanes = slice(128 * (row % 2), 128 * (row % 2 + 1))
            state[GROUND, 2 * j + row // 2 : 2 * j + row // 2 + 1, lanes] = gb[j, row : row + 1, :]
    finish(borders + [middle])
    state[DIAG] = folded(OWN) + state[GROUND]
    for k in range(OWN):
        state[R + k] = folded(k)
        table[core, k, SIDE : SIDE + MID] = state[R + k] / state[DIAG]

    gamma_was = curve_was = None
    for it in range(ITERS):
        mine = table.at[core]
        to_partner = send(mine.at[:, SIDE : SIDE + MID], mine.at[:, SIDE : SIDE + MID], (a_s, a_r), 0, near[0])
        halos = []
        for rc in range(2):
            halos.append(send(mine.at[:, SIDE : 2 * SIDE], mine.at[:, SIDE + MID :], (a_s, a_r), 1 + rc, near[1 + rc]))
            halos.append(send(mine.at[:, MID : SIDE + MID], mine.at[:, :SIDE], (a_s, a_r), 3 + rc, near[3 + rc]))
        total_t[...] = jnp.zeros_like(total_t)
        total_h[...] = jnp.zeros_like(total_h)
        energy[...] = jnp.zeros_like(energy)
        stat_s[it] = jnp.zeros_like(stat_s[it])
        for k in range(OWN):
            u = table[core, k, SIDE : SIDE + MID]
            stat_s[it, core, OWN + k : OWN + k + 1, :] = lanes_of(state[R + k] * u)
            if it:
                stat_s[it, core, 2 * OWN + k : 2 * OWN + k + 1, :] = lanes_of(state[S + k] * u)
        to_partner.wait()
        for c in range(2):
            tables(table, c, tab_h, SIDE, MID)
        loop(0, NY, lambda c: gather_heads(pre, c, tab_h, first_values))
        finish(halos)
        for c in range(2):
            tables(table, c, tab_t, 0, WIN)
        loop(0, NY, lambda c: gather_tails(pre, c, tab_t, first_values, diffs, energy))

        for c in range(2):
            stat_s[it, c, :OWN, :] = energy[OWN * c : OWN * (c + 1), :]
        for k in range(OWN):
            u = table[core, k, SIDE : SIDE + MID]
            stat_s[it, core, k : k + 1, :] += lanes_of(state[GROUND] * u * u)
        slot = 2 * x + core
        copies = []
        for at in range(1, 2 * NX):
            theirs = (core + at % 2) % 2
            copies.append(
                send(stat_s.at[it, theirs], stat_x.at[it, slot], (x_s.at[it], x_r.at[it]), at - 1, along_x[at])
            )
        stat_x[it, slot] = stat_s[it, core]
        loop(0, NY // 2, lambda c: scatter_tails(c, ROWS))
        finish(copies)
        part = stat_x[it, 0]
        for j in range(1, 2 * NX):
            part = part + stat_x[it, j]
        stat_z[it, z] = part
        copies = []
        for j in range(1, NZ):
            here = stat_z.at[it, z]
            copies.append(send(here, here, (z_s.at[it], z_r.at[it]), j - 1, along_z[j - 1]))
        loop(NY // 2, NY, lambda c: scatter_tails(c, ROWS))
        keep_tails(ROWS)
        borders = send_borders(OWN)
        loop(0, NY, lambda c: scatter_heads(c, ROWS))
        keep_heads(ROWS)
        middle = send_middle(OWN)
        finish(copies)
        whole = stat_z[it, 0]
        for j in range(1, NZ):
            whole = whole + stat_z[it, j]
        totals = jnp.sum(whole, axis=1, keepdims=True)
        curve, gamma = totals[:OWN], totals[OWN : 2 * OWN]
        if it:
            beta = gamma / gamma_was
            curve = curve + 2.0 * beta * totals[2 * OWN : 3 * OWN] + beta * beta * curve_was
        alpha = gamma / curve
        finish(borders + [middle])
        for k in range(OWN):
            a = alpha[k : k + 1]
            u = table[core, k, SIDE : SIDE + MID]
            image = folded(k) + state[GROUND] * u
            if it:
                b = beta[k : k + 1]
                direction = u + b * state[PP + k]
                along = image + b * state[S + k]
                state[X + k] = state[X + k] + a * direction
            else:
                direction, along = u, image
                state[X + k] = a * direction
            state[PP + k] = direction
            state[S + k] = along
            rest = state[R + k] - a * along
            state[R + k] = rest
            if it < ITERS - 1:
                table[core, k, SIDE : SIDE + MID] = rest / state[DIAG]
        gamma_was, curve_was = gamma, curve

    for g in range(8):
        for k in range(OWN):
            for half in range(2):
                lanes = slice(LANES * half, LANES * (half + 1))
                tile = slice(2 * g + half, 2 * g + half + 1)
                out_s[g, k : k + 1, lanes] = state[X + k, tile, :]
                out_s[g, OWN + k : OWN + k + 1, lanes] = state[R + k, tile, :]
    copies = []
    for j in range(1, 8):
        to = (grp + j) % 8
        copies.append(send(out_s.at[to], out_r.at[grp], (o_s, o_r), j - 1, group[j - 1]))
    out_r[grp] = out_s[grp]
    finish(copies)
    for g in range(8):
        sol[OWN * g : OWN * (g + 1), :] = out_r[g, :OWN, :]
        res[OWN * g : OWN * (g + 1), :] = out_r[g, OWN : 2 * OWN, :]


def on_device(heads, tails, signs, edge_weights, ground):
    dma = lambda *shape: pltpu.SemaphoreType.DMA(shape)
    vmem = pl.BlockSpec(memory_space=pltpu.VMEM)
    out = jax.ShapeDtypeStruct((K, 512), F)
    scratch = [
        pltpu.VMEM((2, 4, 8, WIDE), F),
        pltpu.VMEM((NY, 4, 8, WIDE), F),
        pltpu.VMEM((NY, 6, 8, WIDE), F),
        pltpu.VMEM((8, 4, 128), F),
        pltpu.VMEM((2, OWN, WIN, LANES), F),
        pltpu.VMEM((2, OWN + 1, WIN, LANES), F),
        pltpu.VMEM((OWN + 1, MID, LANES), F),
        pltpu.VMEM((2, OWN + 1, SIDE, LANES), F),
        pltpu.VMEM((2, OWN + 1, SIDE, LANES), F),
        pltpu.VMEM((NY, ROWS, 8, EC), F),
        pltpu.VMEM((NY, 8, EC), F),
        pltpu.VMEM((8, 128), F),
        pltpu.VMEM((2 * ROWS * WIN, LANES), BF),
        pltpu.VMEM((2 * ROWS * MID, LANES), BF),
        pltpu.VMEM((2 * (ROWS + 1) * WIN, LANES), F),
        pltpu.VMEM((2 * (ROWS + 1) * MID, LANES), F),
        pltpu.VMEM((2 + 4 * OWN, MID, LANES), F),
        pltpu.VMEM((ITERS, 2, 16, 128), F),
        pltpu.VMEM((ITERS, 2 * NX, 16, 128), F),
        pltpu.VMEM((ITERS, NZ, 16, 128), F),
        pltpu.VMEM((8, 8, 512), F),
        pltpu.VMEM((8, 8, 512), F),
    ]
    counts = [(NY - 1,), (7,), (5,), (5,), (ITERS, 2 * NX - 1), (ITERS, NZ - 1), (7,)]
    scratch += [dma(*count) for count in counts for _ in range(2)]
    return pl.pallas_call(
        kernel,
        out_shape=(out, out),
        in_specs=[vmem] * 5,
        out_specs=(vmem, vmem),
        scratch_shapes=scratch,
        compiler_params=pltpu.CompilerParams(
            collective_id=0, has_side_effects=True, vmem_limit_bytes=58 * 2**20
        ),
        name="resistances",
    )(
        heads.reshape(64, 128), tails.reshape(64, 128), edge_weights.reshape(64, 128), signs, ground.reshape(4, 128)
    )


def solution(mesh):
    in_specs = (
        P(("dom", "grp")),
        P(("dom", "grp")),
        P(None, ("dom", "grp")),
        P(("dom", "grp")),
        P(("dom", "grp")),
    )
    out_specs = (P(None, ("dom", "grp")), P(None, ("dom", "grp")))
    return jax.shard_map(
        on_device, mesh=mesh, in_specs=in_specs, out_specs=out_specs, check_vma=False
    )
```

```python
import functools

import jax
import jax.numpy as jnp
from jax import lax
from jax.experimental import pallas as pl
from jax.experimental.pallas import tpu as pltpu
from jax.sharding import PartitionSpec as P

MESH = pl.DeviceIdType.MESH
BF, F, I = jnp.bfloat16, jnp.float32, jnp.int32
NT = (((1,), (1,)), ((), ()))
K = 24
ITERS = 3
NX, NZ, NY = 4, 8, 4
OWN = 3
ROWS = 2 * OWN
LANES = 256
WIN, MID, SIDE = 32, 16, 8
EC = 8192
WIDE = 1024
COL_H, TILE_H, COL_T, TILE_T, WEIGHT, SIGNS = range(6)


def split(value):
    high = value.astype(BF)
    return high, (value - high.astype(F)).astype(BF)


def onehot(index):
    lanes = lax.broadcasted_iota(I, (LANES, index.shape[1]), 0).astype(F).astype(BF)
    return jnp.where(lanes == index.astype(BF), jnp.ones((), BF), jnp.zeros((), BF))


def edge_row(pre, c, name):
    return jnp.concatenate([pre[c, name, q : q + 1, :] for q in range(EC // WIDE)], axis=1)


def at_tile(row, tiles):
    return lax.broadcasted_iota(I, (tiles, row.shape[1]), 0).astype(F) == row


def spread(mask, parts):
    ones = jnp.where(mask, 1.0, 0.0).astype(BF)
    return jnp.concatenate([ones * parts[k][q] for q in range(2) for k in range(len(parts))], axis=0)


def prepare(eb, pre, block):
    for source, col, tile in ((0, COL_H, TILE_H), (1, COL_T, TILE_T)):
        whole = eb[block, source].astype(I)
        pre[block, col] = (whole & (LANES - 1)).astype(F)
        pre[block, tile] = (whole >> 8).astype(F)
    pre[block, WEIGHT] = eb[block, 2]
    pre[block, SIGNS] = eb[block, 3]


def sketch_values(pre, c, shift, diffs):
    weight = edge_row(pre, c, WEIGHT)
    bits = edge_row(pre, c, SIGNS).astype(I) >> shift
    root = jnp.sqrt(weight)
    for k in range(ROWS):
        diffs[c, k : k + 1, :] = jnp.where(((bits >> k) & 1) == 1, root, -root)
    diffs[c, ROWS : ROWS + 1, :] = weight


def gather_heads(pre, c, tab_h, first_values):
    nh = ROWS * MID
    got = jnp.dot(tab_h[...], onehot(edge_row(pre, c, COL_H)), preferred_element_type=F)
    mask = at_tile(edge_row(pre, c, TILE_H), MID)
    for k in range(ROWS):
        rows = got[MID * k : MID * (k + 1)] + got[nh + MID * k : nh + MID * (k + 1)]
        first_values[c, k] = jnp.where(mask, rows, 0.0).reshape(MID // 8, 8, EC).sum(0)


def gather_tails(pre, c, tab_t, first_values, diffs, energy):
    nt = ROWS * WIN
    got = jnp.dot(tab_t[...], onehot(edge_row(pre, c, COL_T)), preferred_element_type=F)
    mask = at_tile(edge_row(pre, c, TILE_T), WIN)
    weight = edge_row(pre, c, WEIGHT)
    for k in range(ROWS):
        rows = got[WIN * k : WIN * (k + 1)] + got[nt + WIN * k : nt + WIN * (k + 1)]
        second = jnp.where(mask, rows, 0.0).reshape(WIN // 8, 8, EC).sum(0)
        gap = jnp.sum(first_values[c, k] - second, axis=0, keepdims=True)
        diff = weight * gap
        diffs[c, k : k + 1, :] = diff
        work = diff * gap
        energy[k : k + 1, :] += sum(work[:, 128 * j : 128 * (j + 1)] for j in range(EC // 128))


def scatter(pre, c, rows, tile, col, tiles, diffs, total):
    parts = [split(diffs[c, k : k + 1, :]) for k in range(rows)]
    total[: 2 * rows * tiles] += lax.dot_general(
        spread(at_tile(edge_row(pre, c, tile), tiles), parts),
        onehot(edge_row(pre, c, col)), NT, preferred_element_type=F,
    )


def tables(table, core, tab, first, tiles):
    n, at = ROWS * tiles, OWN * tiles * core
    high, low = split(table[core, :, first : first + tiles])
    tab[at : at + OWN * tiles] = high.reshape(OWN * tiles, LANES)
    tab[n + at : n + at + OWN * tiles] = low.reshape(OWN * tiles, LANES)


def kernel(
    heads, tails, weights, signs, ground, sol, res,
    eb_s, eb, pre, gb, table, acc, in_mid, in_left, in_right, first_values, diffs, energy,
    tab_t, tab_h, total_t, total_h, state, stat_s, stat_x, stat_z, out_s, out_r,
    ag_s, ag_r, gr_s, gr_r, a_s, a_r, b_s, b_r, x_s, x_r, z_s, z_r, o_s, o_r,
):
    dom, grp = lax.axis_index("dom"), lax.axis_index("grp")
    z, x = dom // NX, dom % NX
    y, core = grp // 2, grp % 2
    other = 1 - core
    left, right = (dom + NX * NZ - 1) % (NX * NZ), (dom + 1) % (NX * NZ)
    near = [(dom, 2 * y + other)]
    near += [(left, 2 * y + (core + rc) % 2) for rc in range(2)]
    near += [(right, 2 * y + (core + rc) % 2) for rc in range(2)]
    group = [(dom, (grp + j) % 8) for j in range(1, 8)]
    along_x = [(z * NX + (x + j) % NX, 2 * y + (core + rc) % 2) for j in range(NX) for rc in range(2)]
    along_z = [(((z + j) % NZ) * NX + x, grp) for j in range(1, NZ)]

    barrier = pltpu.get_barrier_semaphore()
    peers = group + near[1:] + along_x[2:] + along_z
    for peer in peers:
        pl.semaphore_signal(barrier, inc=1, device_id=peer, device_id_type=MESH)

    for word in range(2):
        for j in range(8):
            lanes = slice(128 * j, 128 * (j + 1))
            rows = slice(8 * j, 8 * (j + 1))
            eb_s[word, 0, :, lanes] = heads[rows, :].astype(F)
            eb_s[word, 1, :, lanes] = tails[rows, :].astype(F)
            eb_s[word, 2, :, lanes] = weights[rows, :]
        for row in range(8):
            pieces = [signs[word : word + 1, 128 * (8 * j + row) : 128 * (8 * j + row + 1)] for j in range(8)]
            eb_s[word, 3, row : row + 1, :] = jnp.concatenate(pieces, axis=1).astype(F)
    def loop(first, last, step):
        def body(c, carry):
            step(c)
            return carry

        lax.fori_loop(first, last, body, 0)

    shift = ROWS * (y % 2)

    def scatter_tails(c, rows):
        scatter(pre, c, rows, TILE_T, COL_T, WIN, diffs, total_t)

    def scatter_heads(c, rows):
        scatter(pre, c, rows, TILE_H, COL_H, MID, diffs, total_h)

    def sketch_block(block):
        prepare(eb, pre, block)

        def step(c):
            sketch_values(pre, c, shift, diffs)
            scatter_tails(c, ROWS + 1)

        loop(block, block + 1, step)

    total_t[...] = jnp.zeros_like(total_t)
    total_h[...] = jnp.zeros_like(total_h)
    eb[y] = eb_s[y // 2]
    sketch_block(y)
    loop(y, y + 1, lambda c: scatter_heads(c, ROWS + 1))
    pl.semaphore_wait(barrier, len(peers))

    def send(source, target, sems, at, peer):
        copy = pltpu.make_async_remote_copy(
            src_ref=source, dst_ref=target, send_sem=sems[0].at[at], recv_sem=sems[1].at[at],
            device_id=peer, device_id_type=MESH,
        )
        copy.start()
        return copy

    def finish(copies):
        for copy in copies:
            copy.wait()

    arriving = []
    for j in range(1, NY):
        to = (y + j) % NY
        arriving.append(send(eb_s.at[to // 2], eb.at[y], (ag_s, ag_r), j - 1, (dom, 2 * to + core)))
    grounds = [send(ground, gb.at[grp], (gr_s, gr_r), j - 1, group[j - 1]) for j in range(1, 8)]
    gb[grp] = ground[...]

    def send_borders(rows):
        copies = []
        for rc in range(2):
            theirs = (core + rc) % 2
            copies.append(
                send(acc.at[theirs, :rows, :SIDE], in_right.at[rc, :rows], (b_s, b_r), 1 + rc, near[1 + rc])
            )
            copies.append(
                send(acc.at[theirs, :rows, SIDE + MID :], in_left.at[rc, :rows], (b_s, b_r), 3 + rc, near[3 + rc])
            )
        return copies

    def send_middle(rows):
        return send(acc.at[other, :rows, SIDE : SIDE + MID], in_mid.at[:rows], (b_s, b_r), 0, near[0])

    def folded(k):
        low = in_left[0, k] + in_left[1, k]
        high = in_right[0, k] + in_right[1, k]
        return acc[core, k, SIDE : SIDE + MID] + in_mid[k] + jnp.concatenate([low, high], axis=0)

    def keep_tails(rows):
        n = rows * WIN
        for c in range(2):
            for k in range(OWN + (rows > ROWS)):
                at = WIN * (OWN * c + k if k < OWN else ROWS)
                whole = total_t[at : at + WIN] + total_t[n + at : n + at + WIN]
                acc[c, k] = -whole if k < OWN else whole

    def keep_heads(rows):
        n = rows * MID
        for c in range(2):
            for k in range(OWN + (rows > ROWS)):
                at = MID * (OWN * c + k if k < OWN else ROWS)
                acc[c, k, SIDE : SIDE + MID] += total_h[at : at + MID] + total_h[n + at : n + at + MID]

    def lanes_of(value):
        row = jnp.sum(value, axis=0, keepdims=True)
        return row[:, :128] + row[:, 128:]

    DIAG, GROUND, R, PP, S, X = 0, 1, 2, 2 + OWN, 2 + 2 * OWN, 2 + 3 * OWN

    for j in (1, 3, 2):
        arriving[j - 1].wait()
        sketch_block((y + NY - j) % NY)
    keep_tails(ROWS + 1)
    borders = send_borders(OWN + 1)
    loop(1, NY, lambda j: scatter_heads((y + j) % NY, ROWS + 1))
    keep_heads(ROWS + 1)
    middle = send_middle(OWN + 1)
    finish(grounds)
    for j in range(8):
        for row in range(4):
            lanes = slice(128 * (row % 2), 128 * (row % 2 + 1))
            state[GROUND, 2 * j + row // 2 : 2 * j + row // 2 + 1, lanes] = gb[j, row : row + 1, :]
    finish(borders + [middle])
    state[DIAG] = folded(OWN) + state[GROUND]
    for k in range(OWN):
        state[R + k] = folded(k)
        table[core, k, SIDE : SIDE + MID] = state[R + k] / state[DIAG]

    gamma_was = curve_was = None
    for it in range(ITERS):
        mine = table.at[core]
        halos = []
        for rc in range(2):
            halos.append(send(mine.at[:, SIDE : 2 * SIDE], mine.at[:, SIDE + MID :], (a_s, a_r), 1 + rc, near[1 + rc]))
            halos.append(send(mine.at[:, MID : SIDE + MID], mine.at[:, :SIDE], (a_s, a_r), 3 + rc, near[3 + rc]))
        to_partner = send(mine.at[:, SIDE : SIDE + MID], mine.at[:, SIDE : SIDE + MID], (a_s, a_r), 0, near[0])
        total_t[...] = jnp.zeros_like(total_t)
        total_h[...] = jnp.zeros_like(total_h)
        energy[...] = jnp.zeros_like(energy)
        stat_s[it] = jnp.zeros_like(stat_s[it])
        for k in range(OWN):
            u = table[core, k, SIDE : SIDE + MID]
            stat_s[it, core, OWN + k : OWN + k + 1, :] = lanes_of(state[R + k] * u)
            if it:
                stat_s[it, core, 2 * OWN + k : 2 * OWN + k + 1, :] = lanes_of(state[S + k] * u)
        to_partner.wait()
        for c in range(2):
            tables(table, c, tab_h, SIDE, MID)
        loop(0, NY, lambda c: gather_heads(pre, c, tab_h, first_values))
        finish(halos)
        for c in range(2):
            tables(table, c, tab_t, 0, WIN)
        loop(0, NY, lambda c: gather_tails(pre, c, tab_t, first_values, diffs, energy))

        for c in range(2):
            stat_s[it, c, :OWN, :] = energy[OWN * c : OWN * (c + 1), :]
        for k in range(OWN):
            u = table[core, k, SIDE : SIDE + MID]
            stat_s[it, core, k : k + 1, :] += lanes_of(state[GROUND] * u * u)
        slot = 2 * x + core
        copies = []
        for at in range(1, 2 * NX):
            theirs = (core + at % 2) % 2
            copies.append(
                send(stat_s.at[it, theirs], stat_x.at[it, slot], (x_s.at[it], x_r.at[it]), at - 1, along_x[at])
            )
        stat_x[it, slot] = stat_s[it, core]
        loop(0, NY - 1, lambda c: scatter_tails(c, ROWS))
        finish(copies)
        part = stat_x[it, 0]
        for j in range(1, 2 * NX):
            part = part + stat_x[it, j]
        stat_z[it, z] = part
        copies = []
        for j in range(1, NZ):
            here = stat_z.at[it, z]
            copies.append(send(here, here, (z_s.at[it], z_r.at[it]), j - 1, along_z[j - 1]))
        loop(NY - 1, NY, lambda c: scatter_tails(c, ROWS))
        keep_tails(ROWS)
        borders = send_borders(OWN)
        loop(0, NY, lambda c: scatter_heads(c, ROWS))
        keep_heads(ROWS)
        middle = send_middle(OWN)
        finish(copies)
        whole = stat_z[it, 0]
        for j in range(1, NZ):
            whole = whole + stat_z[it, j]
        totals = jnp.sum(whole, axis=1, keepdims=True)
        curve, gamma = totals[:OWN], totals[OWN : 2 * OWN]
        if it:
            beta = gamma / gamma_was
            curve = curve + 2.0 * beta * totals[2 * OWN : 3 * OWN] + beta * beta * curve_was
        alpha = gamma / curve
        finish(borders + [middle])
        for k in range(OWN):
            a = alpha[k : k + 1]
            u = table[core, k, SIDE : SIDE + MID]
            image = folded(k) + state[GROUND] * u
            if it:
                b = beta[k : k + 1]
                direction = u + b * state[PP + k]
                along = image + b * state[S + k]
                state[X + k] = state[X + k] + a * direction
            else:
                direction, along = u, image
                state[X + k] = a * direction
            state[PP + k] = direction
            state[S + k] = along
            rest = state[R + k] - a * along
            state[R + k] = rest
            if it < ITERS - 1:
                table[core, k, SIDE : SIDE + MID] = rest / state[DIAG]
        gamma_was, curve_was = gamma, curve

    for g in range(8):
        for k in range(OWN):
            for half in range(2):
                lanes = slice(LANES * half, LANES * (half + 1))
                tile = slice(2 * g + half, 2 * g + half + 1)
                out_s[g, k : k + 1, lanes] = state[X + k, tile, :]
                out_s[g, OWN + k : OWN + k + 1, lanes] = state[R + k, tile, :]
    copies = []
    for j in range(1, 8):
        to = (grp + j) % 8
        copies.append(send(out_s.at[to], out_r.at[grp], (o_s, o_r), j - 1, group[j - 1]))
    out_r[grp] = out_s[grp]
    finish(copies)
    for g in range(8):
        sol[OWN * g : OWN * (g + 1), :] = out_r[g, :OWN, :]
        res[OWN * g : OWN * (g + 1), :] = out_r[g, OWN : 2 * OWN, :]


def on_device(heads, tails, signs, edge_weights, ground):
    dma = lambda *shape: pltpu.SemaphoreType.DMA(shape)
    vmem = pl.BlockSpec(memory_space=pltpu.VMEM)
    out = jax.ShapeDtypeStruct((K, 512), F)
    scratch = [
        pltpu.VMEM((2, 4, 8, WIDE), F),
        pltpu.VMEM((NY, 4, 8, WIDE), F),
        pltpu.VMEM((NY, 6, 8, WIDE), F),
        pltpu.VMEM((8, 4, 128), F),
        pltpu.VMEM((2, OWN, WIN, LANES), F),
        pltpu.VMEM((2, OWN + 1, WIN, LANES), F),
        pltpu.VMEM((OWN + 1, MID, LANES), F),
        pltpu.VMEM((2, OWN + 1, SIDE, LANES), F),
        pltpu.VMEM((2, OWN + 1, SIDE, LANES), F),
        pltpu.VMEM((NY, ROWS, 8, EC), F),
        pltpu.VMEM((NY, 8, EC), F),
        pltpu.VMEM((8, 128), F),
        pltpu.VMEM((2 * ROWS * WIN, LANES), BF),
        pltpu.VMEM((2 * ROWS * MID, LANES), BF),
        pltpu.VMEM((2 * (ROWS + 1) * WIN, LANES), F),
        pltpu.VMEM((2 * (ROWS + 1) * MID, LANES), F),
        pltpu.VMEM((2 + 4 * OWN, MID, LANES), F),
        pltpu.VMEM((ITERS, 2, 16, 128), F),
        pltpu.VMEM((ITERS, 2 * NX, 16, 128), F),
        pltpu.VMEM((ITERS, NZ, 16, 128), F),
        pltpu.VMEM((8, 8, 512), F),
        pltpu.VMEM((8, 8, 512), F),
    ]
    counts = [(NY - 1,), (7,), (5,), (5,), (ITERS, 2 * NX - 1), (ITERS, NZ - 1), (7,)]
    scratch += [dma(*count) for count in counts for _ in range(2)]
    return pl.pallas_call(
        kernel,
        out_shape=(out, out),
        in_specs=[vmem] * 5,
        out_specs=(vmem, vmem),
        scratch_shapes=scratch,
        compiler_params=pltpu.CompilerParams(
            collective_id=0, has_side_effects=True, vmem_limit_bytes=58 * 2**20
        ),
        name="resistances",
    )(
        heads.reshape(64, 128), tails.reshape(64, 128), edge_weights.reshape(64, 128), signs, ground.reshape(4, 128)
    )


def solution(mesh):
    in_specs = (
        P(("dom", "grp")),
        P(("dom", "grp")),
        P(None, ("dom", "grp")),
        P(("dom", "grp")),
        P(("dom", "grp")),
    )
    out_specs = (P(None, ("dom", "grp")), P(None, ("dom", "grp")))
    return jax.shard_map(
        on_device, mesh=mesh, in_specs=in_specs, out_specs=out_specs, check_vma=False
    )
```

```python
import functools

import jax
import jax.numpy as jnp
from jax import lax
from jax.experimental import pallas as pl
from jax.experimental.pallas import tpu as pltpu
from jax.sharding import PartitionSpec as P

MESH = pl.DeviceIdType.MESH
BF, F, I = jnp.bfloat16, jnp.float32, jnp.int32
NT = (((1,), (1,)), ((), ()))
K = 24
ITERS = 3
NX, NZ, NY = 4, 8, 4
OWN = 3
ROWS = 2 * OWN
LANES = 256
WIN, MID, SIDE = 32, 16, 8
EC = 8192
HALF = 4096
WIDE = 1024
COL_H, TILE_H, COL_T, TILE_T, WEIGHT, SIGNS = range(6)


def split(value):
    high = value.astype(BF)
    return high, (value - high.astype(F)).astype(BF)


def onehot(index):
    lanes = lax.broadcasted_iota(I, (LANES, index.shape[1]), 0).astype(F).astype(BF)
    return jnp.where(lanes == index.astype(BF), jnp.ones((), BF), jnp.zeros((), BF))


def edge_row(pre, c, name):
    return jnp.concatenate([pre[c, name, q : q + 1, :] for q in range(EC // WIDE)], axis=1)


def half_row(pre, c, name):
    block, first = c // 2, (c % 2) * (HALF // WIDE)
    return jnp.concatenate([pre[block, name, pl.ds(first + q, 1), :] for q in range(HALF // WIDE)], axis=1)


def at_tile(row, tiles):
    return lax.broadcasted_iota(I, (tiles, row.shape[1]), 0).astype(F) == row


def spread(mask, parts):
    ones = jnp.where(mask, 1.0, 0.0).astype(BF)
    return jnp.concatenate([ones * parts[k][q] for q in range(2) for k in range(len(parts))], axis=0)


def prepare(eb, pre, block):
    for source, col, tile in ((0, COL_H, TILE_H), (1, COL_T, TILE_T)):
        whole = eb[block, source].astype(I)
        pre[block, col] = (whole & (LANES - 1)).astype(F)
        pre[block, tile] = (whole >> 8).astype(F)
    pre[block, WEIGHT] = eb[block, 2]
    pre[block, SIGNS] = eb[block, 3]


def sketch_tails(pre, c, shift, ends, total_t):
    weight = half_row(pre, c, WEIGHT)
    bits = half_row(pre, c, SIGNS).astype(I) >> shift
    root = jnp.sqrt(weight)
    parts = []
    for k in range(ROWS):
        value = jnp.where(((bits >> k) & 1) == 1, root, -root)
        ends[c, k : k + 1, :] = value
        parts.append(split(value))
    ends[c, ROWS : ROWS + 1, :] = weight
    parts.append(split(weight))
    hot = onehot(half_row(pre, c, COL_T))
    total_t[...] += lax.dot_general(
        spread(at_tile(half_row(pre, c, TILE_T), WIN), parts), hot, NT, preferred_element_type=F
    )


def sketch_heads(pre, c, ends, total_h):
    parts = [split(ends[c, k : k + 1, :]) for k in range(ROWS + 1)]
    total_h[...] += lax.dot_general(
        spread(at_tile(half_row(pre, c, TILE_H), MID), parts),
        onehot(half_row(pre, c, COL_H)), NT, preferred_element_type=F,
    )


def gather_heads(pre, c, tab_h, first_values):
    nh = ROWS * MID
    got = jnp.dot(tab_h[...], onehot(edge_row(pre, c, COL_H)), preferred_element_type=F)
    mask = at_tile(edge_row(pre, c, TILE_H), MID)
    for k in range(ROWS):
        rows = got[MID * k : MID * (k + 1)] + got[nh + MID * k : nh + MID * (k + 1)]
        first_values[c, k] = jnp.where(mask, rows, 0.0).reshape(MID // 8, 8, EC).sum(0)


def gather_tails(pre, c, tab_t, first_values, diffs, energy):
    nt = ROWS * WIN
    got = jnp.dot(tab_t[...], onehot(edge_row(pre, c, COL_T)), preferred_element_type=F)
    mask = at_tile(edge_row(pre, c, TILE_T), WIN)
    weight = edge_row(pre, c, WEIGHT)
    for k in range(ROWS):
        rows = got[WIN * k : WIN * (k + 1)] + got[nt + WIN * k : nt + WIN * (k + 1)]
        second = jnp.where(mask, rows, 0.0).reshape(WIN // 8, 8, EC).sum(0)
        gap = jnp.sum(first_values[c, k] - second, axis=0, keepdims=True)
        diff = weight * gap
        diffs[c, k : k + 1, :] = diff
        work = diff * gap
        energy[k : k + 1, :] += sum(work[:, 128 * j : 128 * (j + 1)] for j in range(EC // 128))


def scatter(pre, c, rows, tile, col, tiles, diffs, total):
    parts = [split(diffs[c, k : k + 1, :]) for k in range(rows)]
    total[: 2 * rows * tiles] += lax.dot_general(
        spread(at_tile(edge_row(pre, c, tile), tiles), parts),
        onehot(edge_row(pre, c, col)), NT, preferred_element_type=F,
    )


def tables(table, core, tab, first, tiles):
    n, at = ROWS * tiles, OWN * tiles * core
    high, low = split(table[core, :, first : first + tiles])
    tab[at : at + OWN * tiles] = high.reshape(OWN * tiles, LANES)
    tab[n + at : n + at + OWN * tiles] = low.reshape(OWN * tiles, LANES)


def kernel(
    heads, tails, weights, signs, ground, sol, res,
    eb_s, eb, pre, gb, table, acc, in_mid, in_left, in_right, first_values, diffs, ends, energy,
    tab_t, tab_h, total_t, total_h, state, stat_s, stat_x, stat_z, out_s, out_r,
    ag_s, ag_r, gr_s, gr_r, a_s, a_r, b_s, b_r, x_s, x_r, z_s, z_r, o_s, o_r,
):
    dom, grp = lax.axis_index("dom"), lax.axis_index("grp")
    z, x = dom // NX, dom % NX
    y, core = grp // 2, grp % 2
    other = 1 - core
    left, right = (dom + NX * NZ - 1) % (NX * NZ), (dom + 1) % (NX * NZ)
    near = [(dom, 2 * y + other)]
    near += [(left, 2 * y + (core + rc) % 2) for rc in range(2)]
    near += [(right, 2 * y + (core + rc) % 2) for rc in range(2)]
    group = [(dom, (grp + j) % 8) for j in range(1, 8)]
    along_x = [(z * NX + (x + j) % NX, 2 * y + (core + rc) % 2) for j in range(NX) for rc in range(2)]
    along_z = [(((z + j) % NZ) * NX + x, grp) for j in range(1, NZ)]

    barrier = pltpu.get_barrier_semaphore()
    peers = group + near[1:] + along_x[2:] + along_z
    for peer in peers:
        pl.semaphore_signal(barrier, inc=1, device_id=peer, device_id_type=MESH)

    for word in range(2):
        for j in range(8):
            lanes = slice(128 * j, 128 * (j + 1))
            rows = slice(8 * j, 8 * (j + 1))
            eb_s[word, 0, :, lanes] = heads[rows, :].astype(F)
            eb_s[word, 1, :, lanes] = tails[rows, :].astype(F)
            eb_s[word, 2, :, lanes] = weights[rows, :]
        for row in range(8):
            pieces = [signs[word : word + 1, 128 * (8 * j + row) : 128 * (8 * j + row + 1)] for j in range(8)]
            eb_s[word, 3, row : row + 1, :] = jnp.concatenate(pieces, axis=1).astype(F)
    def loop(first, last, step):
        def body(c, carry):
            step(c)
            return carry

        lax.fori_loop(first, last, body, 0)

    shift = ROWS * (y % 2)

    def scatter_tails(c, rows):
        scatter(pre, c, rows, TILE_T, COL_T, WIN, diffs, total_t)

    def scatter_heads(c, rows):
        scatter(pre, c, rows, TILE_H, COL_H, MID, diffs, total_h)

    pl.semaphore_wait(barrier, len(peers))

    def send(source, target, sems, at, peer):
        copy = pltpu.make_async_remote_copy(
            src_ref=source, dst_ref=target, send_sem=sems[0].at[at], recv_sem=sems[1].at[at],
            device_id=peer, device_id_type=MESH,
        )
        copy.start()
        return copy

    def finish(copies):
        for copy in copies:
            copy.wait()

    arriving = []
    for j in range(1, NY):
        to = (y + j) % NY
        arriving.append(send(eb_s.at[to // 2], eb.at[y], (ag_s, ag_r), j - 1, (dom, 2 * to + core)))
    grounds = [send(ground, gb.at[grp], (gr_s, gr_r), j - 1, group[j - 1]) for j in range(1, 8)]
    eb[y] = eb_s[y // 2]
    gb[grp] = ground[...]

    def send_borders(rows):
        copies = []
        for rc in range(2):
            theirs = (core + rc) % 2
            copies.append(
                send(acc.at[theirs, :rows, :SIDE], in_right.at[rc, :rows], (b_s, b_r), 1 + rc, near[1 + rc])
            )
            copies.append(
                send(acc.at[theirs, :rows, SIDE + MID :], in_left.at[rc, :rows], (b_s, b_r), 3 + rc, near[3 + rc])
            )
        return copies

    def send_middle(rows):
        return send(acc.at[other, :rows, SIDE : SIDE + MID], in_mid.at[:rows], (b_s, b_r), 0, near[0])

    def folded(k):
        low = in_left[0, k] + in_left[1, k]
        high = in_right[0, k] + in_right[1, k]
        return acc[core, k, SIDE : SIDE + MID] + in_mid[k] + jnp.concatenate([low, high], axis=0)

    def keep_tails(rows):
        n = rows * WIN
        for c in range(2):
            for k in range(OWN + (rows > ROWS)):
                at = WIN * (OWN * c + k if k < OWN else ROWS)
                whole = total_t[at : at + WIN] + total_t[n + at : n + at + WIN]
                acc[c, k] = -whole if k < OWN else whole

    def keep_heads(rows):
        n = rows * MID
        for c in range(2):
            for k in range(OWN + (rows > ROWS)):
                at = MID * (OWN * c + k if k < OWN else ROWS)
                acc[c, k, SIDE : SIDE + MID] += total_h[at : at + MID] + total_h[n + at : n + at + MID]

    def lanes_of(value):
        row = jnp.sum(value, axis=0, keepdims=True)
        return row[:, :128] + row[:, 128:]

    DIAG, GROUND, R, PP, S, X = 0, 1, 2, 2 + OWN, 2 + 2 * OWN, 2 + 3 * OWN

    total_t[...] = jnp.zeros_like(total_t)
    total_h[...] = jnp.zeros_like(total_h)
    for j in range(NY):
        block = (y + NY - j) % NY
        if j:
            arriving[j - 1].wait()
        prepare(eb, pre, block)
        loop(0, 2, lambda half: sketch_tails(pre, 2 * block + half, shift, ends, total_t))
    keep_tails(ROWS + 1)
    borders = send_borders(OWN + 1)
    loop(0, 2 * NY, lambda c: sketch_heads(pre, c, ends, total_h))
    keep_heads(ROWS + 1)
    middle = send_middle(OWN + 1)
    finish(grounds)
    for j in range(8):
        for row in range(4):
            lanes = slice(128 * (row % 2), 128 * (row % 2 + 1))
            state[GROUND, 2 * j + row // 2 : 2 * j + row // 2 + 1, lanes] = gb[j, row : row + 1, :]
    finish(borders + [middle])
    state[DIAG] = folded(OWN) + state[GROUND]
    for k in range(OWN):
        state[R + k] = folded(k)
        table[core, k, SIDE : SIDE + MID] = state[R + k] / state[DIAG]

    gamma_was = curve_was = None
    for it in range(ITERS):
        mine = table.at[core]
        halos = []
        for rc in range(2):
            halos.append(send(mine.at[:, SIDE : 2 * SIDE], mine.at[:, SIDE + MID :], (a_s, a_r), 1 + rc, near[1 + rc]))
            halos.append(send(mine.at[:, MID : SIDE + MID], mine.at[:, :SIDE], (a_s, a_r), 3 + rc, near[3 + rc]))
        to_partner = send(mine.at[:, SIDE : SIDE + MID], mine.at[:, SIDE : SIDE + MID], (a_s, a_r), 0, near[0])
        total_t[...] = jnp.zeros_like(total_t)
        total_h[...] = jnp.zeros_like(total_h)
        energy[...] = jnp.zeros_like(energy)
        stat_s[it] = jnp.zeros_like(stat_s[it])
        for k in range(OWN):
            u = table[core, k, SIDE : SIDE + MID]
            stat_s[it, core, OWN + k : OWN + k + 1, :] = lanes_of(state[R + k] * u)
            if it:
                stat_s[it, core, 2 * OWN + k : 2 * OWN + k + 1, :] = lanes_of(state[S + k] * u)
        to_partner.wait()
        for c in range(2):
            tables(table, c, tab_h, SIDE, MID)
        loop(0, NY, lambda c: gather_heads(pre, c, tab_h, first_values))
        finish(halos)
        for c in range(2):
            tables(table, c, tab_t, 0, WIN)
        loop(0, NY, lambda c: gather_tails(pre, c, tab_t, first_values, diffs, energy))

        for c in range(2):
            stat_s[it, c, :OWN, :] = energy[OWN * c : OWN * (c + 1), :]
        for k in range(OWN):
            u = table[core, k, SIDE : SIDE + MID]
            stat_s[it, core, k : k + 1, :] += lanes_of(state[GROUND] * u * u)
        slot = 2 * x + core
        copies = []
        for at in range(1, 2 * NX):
            theirs = (core + at % 2) % 2
            copies.append(
                send(stat_s.at[it, theirs], stat_x.at[it, slot], (x_s.at[it], x_r.at[it]), at - 1, along_x[at])
            )
        stat_x[it, slot] = stat_s[it, core]
        loop(0, NY - 1, lambda c: scatter_tails(c, ROWS))
        finish(copies)
        part = stat_x[it, 0]
        for j in range(1, 2 * NX):
            part = part + stat_x[it, j]
        stat_z[it, z] = part
        copies = []
        for j in range(1, NZ):
            here = stat_z.at[it, z]
            copies.append(send(here, here, (z_s.at[it], z_r.at[it]), j - 1, along_z[j - 1]))
        loop(NY - 1, NY, lambda c: scatter_tails(c, ROWS))
        keep_tails(ROWS)
        borders = send_borders(OWN)
        loop(0, NY, lambda c: scatter_heads(c, ROWS))
        keep_heads(ROWS)
        middle = send_middle(OWN)
        finish(copies)
        whole = stat_z[it, 0]
        for j in range(1, NZ):
            whole = whole + stat_z[it, j]
        totals = jnp.sum(whole, axis=1, keepdims=True)
        curve, gamma = totals[:OWN], totals[OWN : 2 * OWN]
        if it:
            beta = gamma / gamma_was
            curve = curve + 2.0 * beta * totals[2 * OWN : 3 * OWN] + beta * beta * curve_was
        alpha = gamma / curve
        finish(borders + [middle])
        for k in range(OWN):
            a = alpha[k : k + 1]
            u = table[core, k, SIDE : SIDE + MID]
            image = folded(k) + state[GROUND] * u
            if it:
                b = beta[k : k + 1]
                direction = u + b * state[PP + k]
                along = image + b * state[S + k]
                state[X + k] = state[X + k] + a * direction
            else:
                direction, along = u, image
                state[X + k] = a * direction
            state[PP + k] = direction
            state[S + k] = along
            rest = state[R + k] - a * along
            state[R + k] = rest
            if it < ITERS - 1:
                table[core, k, SIDE : SIDE + MID] = rest / state[DIAG]
        gamma_was, curve_was = gamma, curve

    for g in range(8):
        for k in range(OWN):
            for half in range(2):
                lanes = slice(LANES * half, LANES * (half + 1))
                tile = slice(2 * g + half, 2 * g + half + 1)
                out_s[g, k : k + 1, lanes] = state[X + k, tile, :]
                out_s[g, OWN + k : OWN + k + 1, lanes] = state[R + k, tile, :]
    copies = []
    for j in range(1, 8):
        to = (grp + j) % 8
        copies.append(send(out_s.at[to], out_r.at[grp], (o_s, o_r), j - 1, group[j - 1]))
    out_r[grp] = out_s[grp]
    finish(copies)
    for g in range(8):
        sol[OWN * g : OWN * (g + 1), :] = out_r[g, :OWN, :]
        res[OWN * g : OWN * (g + 1), :] = out_r[g, OWN : 2 * OWN, :]


def on_device(heads, tails, signs, edge_weights, ground):
    dma = lambda *shape: pltpu.SemaphoreType.DMA(shape)
    vmem = pl.BlockSpec(memory_space=pltpu.VMEM)
    out = jax.ShapeDtypeStruct((K, 512), F)
    scratch = [
        pltpu.VMEM((2, 4, 8, WIDE), F),
        pltpu.VMEM((NY, 4, 8, WIDE), F),
        pltpu.VMEM((NY, 6, 8, WIDE), F),
        pltpu.VMEM((8, 4, 128), F),
        pltpu.VMEM((2, OWN, WIN, LANES), F),
        pltpu.VMEM((2, OWN + 1, WIN, LANES), F),
        pltpu.VMEM((OWN + 1, MID, LANES), F),
        pltpu.VMEM((2, OWN + 1, SIDE, LANES), F),
        pltpu.VMEM((2, OWN + 1, SIDE, LANES), F),
        pltpu.VMEM((NY, ROWS, 8, EC), F),
        pltpu.VMEM((NY, 8, EC), F),
        pltpu.VMEM((2 * NY, 8, HALF), F),
        pltpu.VMEM((8, 128), F),
        pltpu.VMEM((2 * ROWS * WIN, LANES), BF),
        pltpu.VMEM((2 * ROWS * MID, LANES), BF),
        pltpu.VMEM((2 * (ROWS + 1) * WIN, LANES), F),
        pltpu.VMEM((2 * (ROWS + 1) * MID, LANES), F),
        pltpu.VMEM((2 + 4 * OWN, MID, LANES), F),
        pltpu.VMEM((ITERS, 2, 16, 128), F),
        pltpu.VMEM((ITERS, 2 * NX, 16, 128), F),
        pltpu.VMEM((ITERS, NZ, 16, 128), F),
        pltpu.VMEM((8, 8, 512), F),
        pltpu.VMEM((8, 8, 512), F),
    ]
    counts = [(NY - 1,), (7,), (5,), (5,), (ITERS, 2 * NX - 1), (ITERS, NZ - 1), (7,)]
    scratch += [dma(*count) for count in counts for _ in range(2)]
    return pl.pallas_call(
        kernel,
        out_shape=(out, out),
        in_specs=[vmem] * 5,
        out_specs=(vmem, vmem),
        scratch_shapes=scratch,
        compiler_params=pltpu.CompilerParams(
            collective_id=0, has_side_effects=True, vmem_limit_bytes=58 * 2**20
        ),
        name="resistances",
    )(
        heads.reshape(64, 128), tails.reshape(64, 128), edge_weights.reshape(64, 128), signs, ground.reshape(4, 128)
    )


def solution(mesh):
    in_specs = (
        P(("dom", "grp")),
        P(("dom", "grp")),
        P(None, ("dom", "grp")),
        P(("dom", "grp")),
        P(("dom", "grp")),
    )
    out_specs = (P(None, ("dom", "grp")), P(None, ("dom", "grp")))
    return jax.shard_map(
        on_device, mesh=mesh, in_specs=in_specs, out_specs=out_specs, check_vma=False
    )
```

```python
import functools

import jax
import jax.numpy as jnp
from jax import lax
from jax.experimental import pallas as pl
from jax.experimental.pallas import tpu as pltpu
from jax.sharding import PartitionSpec as P

MESH = pl.DeviceIdType.MESH
BF, F, I = jnp.bfloat16, jnp.float32, jnp.int32
NT = (((1,), (1,)), ((), ()))
K = 24
ITERS = 3
NX, NZ, NY = 4, 8, 4
OWN = 3
ROWS = 2 * OWN
LANES = 256
WIN, MID, SIDE = 32, 16, 8
EC = 8192
HALF = 4096
WIDE = 1024
COL_H, TILE_H, COL_T, TILE_T, WEIGHT, SIGNS = range(6)


def split(value):
    high = value.astype(BF)
    return high, (value - high.astype(F)).astype(BF)


def onehot(index):
    lanes = lax.broadcasted_iota(I, (LANES, index.shape[1]), 0).astype(F).astype(BF)
    return jnp.where(lanes == index.astype(BF), jnp.ones((), BF), jnp.zeros((), BF))


def edge_row(pre, c, name):
    return jnp.concatenate([pre[c, name, q : q + 1, :] for q in range(EC // WIDE)], axis=1)


def half_row(pre, c, name):
    block, first = c // 2, (c % 2) * (HALF // WIDE)
    return jnp.concatenate([pre[block, name, pl.ds(first + q, 1), :] for q in range(HALF // WIDE)], axis=1)


def at_tile(row, tiles):
    return lax.broadcasted_iota(I, (tiles, row.shape[1]), 0).astype(F) == row


def spread(mask, parts):
    ones = jnp.where(mask, 1.0, 0.0).astype(BF)
    return jnp.concatenate([ones * parts[k][q] for q in range(2) for k in range(len(parts))], axis=0)


def prepare(eb, pre, block):
    for source, col, tile in ((0, COL_H, TILE_H), (1, COL_T, TILE_T)):
        whole = eb[block, source].astype(I)
        pre[block, col] = (whole & (LANES - 1)).astype(F)
        pre[block, tile] = (whole >> 8).astype(F)
    pre[block, WEIGHT] = eb[block, 2]
    pre[block, SIGNS] = eb[block, 3]


def sketch_tails(pre, c, shift, ends, total_t):
    weight = half_row(pre, c, WEIGHT)
    bits = half_row(pre, c, SIGNS).astype(I) >> shift
    root = jnp.sqrt(weight)
    parts = []
    for k in range(ROWS):
        value = jnp.where(((bits >> k) & 1) == 1, root, -root)
        ends[c, k : k + 1, :] = value
        parts.append(split(value))
    ends[c, ROWS : ROWS + 1, :] = weight
    parts.append(split(weight))
    hot = onehot(half_row(pre, c, COL_T))
    total_t[...] += lax.dot_general(
        spread(at_tile(half_row(pre, c, TILE_T), WIN), parts), hot, NT, preferred_element_type=F
    )


def sketch_heads(pre, c, ends, total_h):
    parts = [split(ends[c, k : k + 1, :]) for k in range(ROWS + 1)]
    total_h[...] += lax.dot_general(
        spread(at_tile(half_row(pre, c, TILE_H), MID), parts),
        onehot(half_row(pre, c, COL_H)), NT, preferred_element_type=F,
    )


def gather_heads(pre, c, tab_h, first_values):
    nh = ROWS * MID
    got = jnp.dot(tab_h[...], onehot(edge_row(pre, c, COL_H)), preferred_element_type=F)
    mask = at_tile(edge_row(pre, c, TILE_H), MID)
    for k in range(ROWS):
        rows = got[MID * k : MID * (k + 1)] + got[nh + MID * k : nh + MID * (k + 1)]
        first_values[c, k] = jnp.where(mask, rows, 0.0).reshape(MID // 8, 8, EC).sum(0)


def gather_tails(pre, c, tab_t, first_values, diffs, energy):
    nt = ROWS * WIN
    got = jnp.dot(tab_t[...], onehot(edge_row(pre, c, COL_T)), preferred_element_type=F)
    mask = at_tile(edge_row(pre, c, TILE_T), WIN)
    weight = edge_row(pre, c, WEIGHT)
    for k in range(ROWS):
        rows = got[WIN * k : WIN * (k + 1)] + got[nt + WIN * k : nt + WIN * (k + 1)]
        second = jnp.where(mask, rows, 0.0).reshape(WIN // 8, 8, EC).sum(0)
        gap = jnp.sum(first_values[c, k] - second, axis=0, keepdims=True)
        diff = weight * gap
        diffs[c, k : k + 1, :] = diff
        work = diff * gap
        energy[k : k + 1, :] += sum(work[:, 128 * j : 128 * (j + 1)] for j in range(EC // 128))


def scatter(pre, c, rows, tile, col, tiles, diffs, total):
    parts = [split(diffs[c, k : k + 1, :]) for k in range(rows)]
    total[: 2 * rows * tiles] += lax.dot_general(
        spread(at_tile(edge_row(pre, c, tile), tiles), parts),
        onehot(edge_row(pre, c, col)), NT, preferred_element_type=F,
    )


def tables(table, core, tab, first, tiles):
    n, at = ROWS * tiles, OWN * tiles * core
    high, low = split(table[core, :, first : first + tiles])
    tab[at : at + OWN * tiles] = high.reshape(OWN * tiles, LANES)
    tab[n + at : n + at + OWN * tiles] = low.reshape(OWN * tiles, LANES)


def kernel(
    heads, tails, weights, signs, ground, sol, res,
    eb_s, eb, pre, gb, table, acc, in_mid, in_left, in_right, first_values, diffs, ends, energy,
    tab_t, tab_h, total_t, total_h, state, stat_s, stat_x, stat_z, out_s, out_r,
    ag_s, ag_r, gr_s, gr_r, a_s, a_r, b_s, b_r, x_s, x_r, z_s, z_r, o_s, o_r,
):
    dom, grp = lax.axis_index("dom"), lax.axis_index("grp")
    z, x = dom // NX, dom % NX
    y, core = grp // 2, grp % 2
    other = 1 - core
    left, right = (dom + NX * NZ - 1) % (NX * NZ), (dom + 1) % (NX * NZ)
    near = [(dom, 2 * y + other)]
    near += [(left, 2 * y + (core + rc) % 2) for rc in range(2)]
    near += [(right, 2 * y + (core + rc) % 2) for rc in range(2)]
    group = [(dom, (grp + j) % 8) for j in range(1, 8)]
    along_x = [(z * NX + (x + j) % NX, 2 * y + (core + rc) % 2) for j in range(NX) for rc in range(2)]
    along_z = [(((z + j) % NZ) * NX + x, grp) for j in range(1, NZ)]

    barrier = pltpu.get_barrier_semaphore()
    peers = group + near[1:] + along_x[2:] + along_z
    for peer in peers:
        pl.semaphore_signal(barrier, inc=1, device_id=peer, device_id_type=MESH)

    for word in range(2):
        for j in range(8):
            lanes = slice(128 * j, 128 * (j + 1))
            rows = slice(8 * j, 8 * (j + 1))
            eb_s[word, 0, :, lanes] = heads[rows, :].astype(F)
            eb_s[word, 1, :, lanes] = tails[rows, :].astype(F)
            eb_s[word, 2, :, lanes] = weights[rows, :]
        for row in range(8):
            pieces = [signs[word : word + 1, 128 * (8 * j + row) : 128 * (8 * j + row + 1)] for j in range(8)]
            eb_s[word, 3, row : row + 1, :] = jnp.concatenate(pieces, axis=1).astype(F)
    def loop(first, last, step):
        def body(c, carry):
            step(c)
            return carry

        lax.fori_loop(first, last, body, 0)

    shift = ROWS * (y % 2)

    def scatter_tails(c, rows):
        scatter(pre, c, rows, TILE_T, COL_T, WIN, diffs, total_t)

    def scatter_heads(c, rows):
        scatter(pre, c, rows, TILE_H, COL_H, MID, diffs, total_h)

    pl.semaphore_wait(barrier, len(peers))

    def send(source, target, sems, at, peer):
        copy = pltpu.make_async_remote_copy(
            src_ref=source, dst_ref=target, send_sem=sems[0].at[at], recv_sem=sems[1].at[at],
            device_id=peer, device_id_type=MESH,
        )
        copy.start()
        return copy

    def finish(copies):
        for copy in copies:
            copy.wait()

    def block_copy(j):
        to = (y + j) % NY
        return pltpu.make_async_remote_copy(
            src_ref=eb_s.at[to // 2], dst_ref=eb.at[y], send_sem=ag_s.at[j - 1], recv_sem=ag_r.at[j - 1],
            device_id=(dom, 2 * to + core), device_id_type=MESH,
        )

    for j in range(1, NY):
        block_copy(j).start()
    grounds = [send(ground, gb.at[grp], (gr_s, gr_r), j - 1, group[j - 1]) for j in range(1, 8)]
    eb[y] = eb_s[y // 2]
    gb[grp] = ground[...]

    def send_borders(rows):
        copies = []
        for rc in range(2):
            theirs = (core + rc) % 2
            copies.append(
                send(acc.at[theirs, :rows, :SIDE], in_right.at[rc, :rows], (b_s, b_r), 1 + rc, near[1 + rc])
            )
            copies.append(
                send(acc.at[theirs, :rows, SIDE + MID :], in_left.at[rc, :rows], (b_s, b_r), 3 + rc, near[3 + rc])
            )
        return copies

    def send_middle(rows):
        return send(acc.at[other, :rows, SIDE : SIDE + MID], in_mid.at[:rows], (b_s, b_r), 0, near[0])

    def folded(k):
        low = in_left[0, k] + in_left[1, k]
        high = in_right[0, k] + in_right[1, k]
        return acc[core, k, SIDE : SIDE + MID] + in_mid[k] + jnp.concatenate([low, high], axis=0)

    def keep_tails(rows):
        n = rows * WIN
        for c in range(2):
            for k in range(OWN + (rows > ROWS)):
                at = WIN * (OWN * c + k if k < OWN else ROWS)
                whole = total_t[at : at + WIN] + total_t[n + at : n + at + WIN]
                acc[c, k] = -whole if k < OWN else whole

    def keep_heads(rows):
        n = rows * MID
        for c in range(2):
            for k in range(OWN + (rows > ROWS)):
                at = MID * (OWN * c + k if k < OWN else ROWS)
                acc[c, k, SIDE : SIDE + MID] += total_h[at : at + MID] + total_h[n + at : n + at + MID]

    def lanes_of(value):
        row = jnp.sum(value, axis=0, keepdims=True)
        return row[:, :128] + row[:, 128:]

    DIAG, GROUND, R, PP, S, X = 0, 1, 2, 2 + OWN, 2 + 2 * OWN, 2 + 3 * OWN

    total_t[...] = jnp.zeros_like(total_t)
    total_h[...] = jnp.zeros_like(total_h)

    def sketch_block(j):
        block = (y + NY - j) % NY

        @pl.when(j > 0)
        def _():
            block_copy(j).wait()

        prepare(eb, pre, block)
        loop(0, 2, lambda half: sketch_tails(pre, 2 * block + half, shift, ends, total_t))

    loop(0, NY, sketch_block)
    keep_tails(ROWS + 1)
    borders = send_borders(OWN + 1)
    loop(0, 2 * NY, lambda c: sketch_heads(pre, c, ends, total_h))
    keep_heads(ROWS + 1)
    middle = send_middle(OWN + 1)
    finish(grounds)
    for j in range(8):
        for row in range(4):
            lanes = slice(128 * (row % 2), 128 * (row % 2 + 1))
            state[GROUND, 2 * j + row // 2 : 2 * j + row // 2 + 1, lanes] = gb[j, row : row + 1, :]
    finish(borders + [middle])
    state[DIAG] = folded(OWN) + state[GROUND]
    for k in range(OWN):
        state[R + k] = folded(k)
        table[core, k, SIDE : SIDE + MID] = state[R + k] / state[DIAG]

    state[PP:] = jnp.zeros_like(state[PP:])

    def iterate(it, carry):
        gamma_was, curve_was = carry
        mine = table.at[core]
        halos = []
        for rc in range(2):
            halos.append(send(mine.at[:, SIDE : 2 * SIDE], mine.at[:, SIDE + MID :], (a_s, a_r), 1 + rc, near[1 + rc]))
            halos.append(send(mine.at[:, MID : SIDE + MID], mine.at[:, :SIDE], (a_s, a_r), 3 + rc, near[3 + rc]))
        to_partner = send(mine.at[:, SIDE : SIDE + MID], mine.at[:, SIDE : SIDE + MID], (a_s, a_r), 0, near[0])
        total_t[...] = jnp.zeros_like(total_t)
        total_h[...] = jnp.zeros_like(total_h)
        energy[...] = jnp.zeros_like(energy)
        stat_s[it] = jnp.zeros_like(stat_s[it])
        for k in range(OWN):
            u = table[core, k, SIDE : SIDE + MID]
            stat_s[it, core, OWN + k : OWN + k + 1, :] = lanes_of(state[R + k] * u)
            stat_s[it, core, 2 * OWN + k : 2 * OWN + k + 1, :] = lanes_of(state[S + k] * u)
        to_partner.wait()
        for c in range(2):
            tables(table, c, tab_h, SIDE, MID)
        loop(0, NY, lambda c: gather_heads(pre, c, tab_h, first_values))
        finish(halos)
        for c in range(2):
            tables(table, c, tab_t, 0, WIN)
        loop(0, NY, lambda c: gather_tails(pre, c, tab_t, first_values, diffs, energy))

        for c in range(2):
            stat_s[it, c, :OWN, :] = energy[OWN * c : OWN * (c + 1), :]
        for k in range(OWN):
            u = table[core, k, SIDE : SIDE + MID]
            stat_s[it, core, k : k + 1, :] += lanes_of(state[GROUND] * u * u)
        slot = 2 * x + core
        copies = []
        for at in range(1, 2 * NX):
            theirs = (core + at % 2) % 2
            copies.append(
                send(stat_s.at[it, theirs], stat_x.at[it, slot], (x_s.at[it], x_r.at[it]), at - 1, along_x[at])
            )
        stat_x[it, slot] = stat_s[it, core]
        loop(0, NY - 1, lambda c: scatter_tails(c, ROWS))
        finish(copies)
        part = stat_x[it, 0]
        for j in range(1, 2 * NX):
            part = part + stat_x[it, j]
        stat_z[it, z] = part
        copies = []
        for j in range(1, NZ):
            here = stat_z.at[it, z]
            copies.append(send(here, here, (z_s.at[it], z_r.at[it]), j - 1, along_z[j - 1]))
        loop(NY - 1, NY, lambda c: scatter_tails(c, ROWS))
        keep_tails(ROWS)
        borders = send_borders(OWN)
        loop(0, NY, lambda c: scatter_heads(c, ROWS))
        keep_heads(ROWS)
        middle = send_middle(OWN)
        finish(copies)
        whole = stat_z[it, 0]
        for j in range(1, NZ):
            whole = whole + stat_z[it, j]
        totals = jnp.sum(whole, axis=1, keepdims=True)
        curve, gamma = totals[:OWN], totals[OWN : 2 * OWN]
        beta = jnp.where(it > 0, gamma / gamma_was, 0.0)
        curve = curve + 2.0 * beta * totals[2 * OWN : 3 * OWN] + beta * beta * curve_was
        alpha = gamma / curve
        finish(borders + [middle])
        for k in range(OWN):
            a = alpha[k : k + 1]
            u = table[core, k, SIDE : SIDE + MID]
            image = folded(k) + state[GROUND] * u
            b = beta[k : k + 1]
            direction = u + b * state[PP + k]
            along = image + b * state[S + k]
            state[X + k] = state[X + k] + a * direction
            state[PP + k] = direction
            state[S + k] = along
            rest = state[R + k] - a * along
            state[R + k] = rest
            table[core, k, SIDE : SIDE + MID] = rest / state[DIAG]
        return gamma, curve

    lax.fori_loop(0, ITERS, iterate, (jnp.ones((OWN, 1), F), jnp.zeros((OWN, 1), F)))

    for g in range(8):
        for k in range(OWN):
            for half in range(2):
                lanes = slice(LANES * half, LANES * (half + 1))
                tile = slice(2 * g + half, 2 * g + half + 1)
                out_s[g, k : k + 1, lanes] = state[X + k, tile, :]
                out_s[g, OWN + k : OWN + k + 1, lanes] = state[R + k, tile, :]
    copies = []
    for j in range(1, 8):
        to = (grp + j) % 8
        copies.append(send(out_s.at[to], out_r.at[grp], (o_s, o_r), j - 1, group[j - 1]))
    out_r[grp] = out_s[grp]
    finish(copies)
    for g in range(8):
        sol[OWN * g : OWN * (g + 1), :] = out_r[g, :OWN, :]
        res[OWN * g : OWN * (g + 1), :] = out_r[g, OWN : 2 * OWN, :]


def on_device(heads, tails, signs, edge_weights, ground):
    dma = lambda *shape: pltpu.SemaphoreType.DMA(shape)
    vmem = pl.BlockSpec(memory_space=pltpu.VMEM)
    out = jax.ShapeDtypeStruct((K, 512), F)
    scratch = [
        pltpu.VMEM((2, 4, 8, WIDE), F),
        pltpu.VMEM((NY, 4, 8, WIDE), F),
        pltpu.VMEM((NY, 6, 8, WIDE), F),
        pltpu.VMEM((8, 4, 128), F),
        pltpu.VMEM((2, OWN, WIN, LANES), F),
        pltpu.VMEM((2, OWN + 1, WIN, LANES), F),
        pltpu.VMEM((OWN + 1, MID, LANES), F),
        pltpu.VMEM((2, OWN + 1, SIDE, LANES), F),
        pltpu.VMEM((2, OWN + 1, SIDE, LANES), F),
        pltpu.VMEM((NY, ROWS, 8, EC), F),
        pltpu.VMEM((NY, 8, EC), F),
        pltpu.VMEM((2 * NY, 8, HALF), F),
        pltpu.VMEM((8, 128), F),
        pltpu.VMEM((2 * ROWS * WIN, LANES), BF),
        pltpu.VMEM((2 * ROWS * MID, LANES), BF),
        pltpu.VMEM((2 * (ROWS + 1) * WIN, LANES), F),
        pltpu.VMEM((2 * (ROWS + 1) * MID, LANES), F),
        pltpu.VMEM((2 + 4 * OWN, MID, LANES), F),
        pltpu.VMEM((ITERS, 2, 16, 128), F),
        pltpu.VMEM((ITERS, 2 * NX, 16, 128), F),
        pltpu.VMEM((ITERS, NZ, 16, 128), F),
        pltpu.VMEM((8, 8, 512), F),
        pltpu.VMEM((8, 8, 512), F),
    ]
    counts = [(NY - 1,), (7,), (5,), (5,), (ITERS, 2 * NX - 1), (ITERS, NZ - 1), (7,)]
    scratch += [dma(*count) for count in counts for _ in range(2)]
    return pl.pallas_call(
        kernel,
        out_shape=(out, out),
        in_specs=[vmem] * 5,
        out_specs=(vmem, vmem),
        scratch_shapes=scratch,
        compiler_params=pltpu.CompilerParams(
            collective_id=0, has_side_effects=True, vmem_limit_bytes=58 * 2**20
        ),
        name="resistances",
    )(
        heads.reshape(64, 128), tails.reshape(64, 128), edge_weights.reshape(64, 128), signs, ground.reshape(4, 128)
    )


def solution(mesh):
    in_specs = (
        P(("dom", "grp")),
        P(("dom", "grp")),
        P(None, ("dom", "grp")),
        P(("dom", "grp")),
        P(("dom", "grp")),
    )
    out_specs = (P(None, ("dom", "grp")), P(None, ("dom", "grp")))
    return jax.shard_map(
        on_device, mesh=mesh, in_specs=in_specs, out_specs=out_specs, check_vma=False
    )
```

```python
import functools

import jax
import jax.numpy as jnp
from jax import lax
from jax.experimental import pallas as pl
from jax.experimental.pallas import tpu as pltpu
from jax.sharding import PartitionSpec as P

MESH = pl.DeviceIdType.MESH
BF, F, I = jnp.bfloat16, jnp.float32, jnp.int32
NT = (((1,), (1,)), ((), ()))
K = 24
ITERS = 3
NX, NZ, NY = 4, 8, 4
OWN = 3
ROWS = 2 * OWN
LANES = 256
WIN, MID, SIDE = 32, 16, 8
EC = 8192
HALF = 4096
WIDE = 1024
COL_H, TILE_H, COL_T, TILE_T, WEIGHT, SIGNS = range(6)


def split(value):
    high = value.astype(BF)
    return high, (value - high.astype(F)).astype(BF)


def onehot(index):
    lanes = lax.broadcasted_iota(I, (LANES, index.shape[1]), 0).astype(F).astype(BF)
    return jnp.where(lanes == index.astype(BF), jnp.ones((), BF), jnp.zeros((), BF))


def edge_row(pre, c, name):
    return jnp.concatenate([pre[c, name, q : q + 1, :] for q in range(EC // WIDE)], axis=1)


def half_row(pre, c, name):
    block, first = c // 2, (c % 2) * (HALF // WIDE)
    return jnp.concatenate([pre[block, name, pl.ds(first + q, 1), :] for q in range(HALF // WIDE)], axis=1)


def at_tile(row, tiles):
    return lax.broadcasted_iota(I, (tiles, row.shape[1]), 0).astype(F) == row


def spread(mask, parts):
    ones = jnp.where(mask, 1.0, 0.0).astype(BF)
    return jnp.concatenate([ones * parts[k][q] for q in range(2) for k in range(len(parts))], axis=0)


def prepare(eb, pre, block):
    for source, col, tile in ((0, COL_H, TILE_H), (1, COL_T, TILE_T)):
        whole = eb[block, source].astype(I)
        pre[block, col] = (whole & (LANES - 1)).astype(F)
        pre[block, tile] = (whole >> 8).astype(F)
    pre[block, WEIGHT] = eb[block, 2]
    pre[block, SIGNS] = eb[block, 3]


def sketch_tails(pre, c, shift, ends, total_t):
    weight = half_row(pre, c, WEIGHT)
    bits = half_row(pre, c, SIGNS).astype(I) >> shift
    root = jnp.sqrt(weight)
    parts = []
    for k in range(ROWS):
        value = jnp.where(((bits >> k) & 1) == 1, root, -root)
        ends[c, k : k + 1, :] = value
        parts.append(split(value))
    ends[c, ROWS : ROWS + 1, :] = weight
    parts.append(split(weight))
    hot = onehot(half_row(pre, c, COL_T))
    total_t[...] += lax.dot_general(
        spread(at_tile(half_row(pre, c, TILE_T), WIN), parts), hot, NT, preferred_element_type=F
    )


def sketch_heads(pre, c, ends, total_h):
    parts = [split(ends[c, k : k + 1, :]) for k in range(ROWS + 1)]
    total_h[...] += lax.dot_general(
        spread(at_tile(half_row(pre, c, TILE_H), MID), parts),
        onehot(half_row(pre, c, COL_H)), NT, preferred_element_type=F,
    )


def gather_heads(pre, c, tab_h, first_values):
    nh = ROWS * MID
    got = jnp.dot(tab_h[...], onehot(edge_row(pre, c, COL_H)), preferred_element_type=F)
    mask = at_tile(edge_row(pre, c, TILE_H), MID)
    for k in range(ROWS):
        rows = got[MID * k : MID * (k + 1)] + got[nh + MID * k : nh + MID * (k + 1)]
        first_values[c, k] = jnp.where(mask, rows, 0.0).reshape(MID // 8, 8, EC).sum(0)


def gather_tails(pre, c, tab_t, first_values, diffs, energy):
    nt = ROWS * WIN
    got = jnp.dot(tab_t[...], onehot(edge_row(pre, c, COL_T)), preferred_element_type=F)
    mask = at_tile(edge_row(pre, c, TILE_T), WIN)
    weight = edge_row(pre, c, WEIGHT)
    for k in range(ROWS):
        rows = got[WIN * k : WIN * (k + 1)] + got[nt + WIN * k : nt + WIN * (k + 1)]
        second = jnp.where(mask, rows, 0.0).reshape(WIN // 8, 8, EC).sum(0)
        gap = jnp.sum(first_values[c, k] - second, axis=0, keepdims=True)
        diff = weight * gap
        diffs[c, k : k + 1, :] = diff
        work = diff * gap
        energy[k : k + 1, :] += sum(work[:, 128 * j : 128 * (j + 1)] for j in range(EC // 128))


def scatter(pre, c, rows, tile, col, tiles, diffs, total):
    parts = [split(diffs[c, k : k + 1, :]) for k in range(rows)]
    total[: 2 * rows * tiles] += lax.dot_general(
        spread(at_tile(edge_row(pre, c, tile), tiles), parts),
        onehot(edge_row(pre, c, col)), NT, preferred_element_type=F,
    )


def tables(table, core, tab, first, tiles):
    n, at = ROWS * tiles, OWN * tiles * core
    high, low = split(table[core, :, first : first + tiles])
    tab[at : at + OWN * tiles] = high.reshape(OWN * tiles, LANES)
    tab[n + at : n + at + OWN * tiles] = low.reshape(OWN * tiles, LANES)


def kernel(
    heads, tails, weights, signs, ground, sol, res,
    eb_s, eb, pre, gb, table, acc, in_mid, in_left, in_right, first_values, diffs, ends, energy,
    tab_t, tab_h, total_t, total_h, state, stat_s, stat_x, stat_z, out_s, out_r,
    ag_s, ag_r, gr_s, gr_r, a_s, a_r, b_s, b_r, x_s, x_r, z_s, z_r, o_s, o_r,
):
    dom, grp = lax.axis_index("dom"), lax.axis_index("grp")
    z, x = dom // NX, dom % NX
    y, core = grp // 2, grp % 2
    other = 1 - core
    left, right = (dom + NX * NZ - 1) % (NX * NZ), (dom + 1) % (NX * NZ)
    near = [(dom, 2 * y + other)]
    near += [(left, 2 * y + (core + rc) % 2) for rc in range(2)]
    near += [(right, 2 * y + (core + rc) % 2) for rc in range(2)]
    group = [(dom, (grp + j) % 8) for j in range(1, 8)]
    along_x = [(z * NX + (x + j) % NX, 2 * y + (core + rc) % 2) for j in range(NX) for rc in range(2)]
    along_z = [(((z + j) % NZ) * NX + x, grp) for j in range(1, NZ)]

    barrier = pltpu.get_barrier_semaphore()
    peers = group + near[1:] + along_x[2:] + along_z
    for peer in peers:
        pl.semaphore_signal(barrier, inc=1, device_id=peer, device_id_type=MESH)

    for word in range(2):
        for j in range(8):
            lanes = slice(128 * j, 128 * (j + 1))
            rows = slice(8 * j, 8 * (j + 1))
            eb_s[word, 0, :, lanes] = heads[rows, :].astype(F)
            eb_s[word, 1, :, lanes] = tails[rows, :].astype(F)
            eb_s[word, 2, :, lanes] = weights[rows, :]
        for row in range(8):
            pieces = [signs[word : word + 1, 128 * (8 * j + row) : 128 * (8 * j + row + 1)] for j in range(8)]
            eb_s[word, 3, row : row + 1, :] = jnp.concatenate(pieces, axis=1).astype(F)
    def loop(first, last, step):
        def body(c, carry):
            step(c)
            return carry

        lax.fori_loop(first, last, body, 0)

    shift = ROWS * (y % 2)

    def scatter_tails(c, rows):
        scatter(pre, c, rows, TILE_T, COL_T, WIN, diffs, total_t)

    def scatter_heads(c, rows):
        scatter(pre, c, rows, TILE_H, COL_H, MID, diffs, total_h)

    pl.semaphore_wait(barrier, len(peers))

    def send(source, target, sems, at, peer):
        copy = pltpu.make_async_remote_copy(
            src_ref=source, dst_ref=target, send_sem=sems[0].at[at], recv_sem=sems[1].at[at],
            device_id=peer, device_id_type=MESH,
        )
        copy.start()
        return copy

    def finish(copies):
        for copy in copies:
            copy.wait()

    def block_copy(j):
        to = (y + j) % NY
        return pltpu.make_async_remote_copy(
            src_ref=eb_s.at[to // 2], dst_ref=eb.at[y], send_sem=ag_s.at[j - 1], recv_sem=ag_r.at[j - 1],
            device_id=(dom, 2 * to + core), device_id_type=MESH,
        )

    for j in range(1, NY):
        block_copy(j).start()
    grounds = [send(ground, gb.at[grp], (gr_s, gr_r), j - 1, group[j - 1]) for j in range(1, 8)]
    eb[y] = eb_s[y // 2]
    gb[grp] = ground[...]

    def send_borders(rows):
        copies = []
        for rc in range(2):
            theirs = (core + rc) % 2
            copies.append(
                send(acc.at[theirs, :rows, :SIDE], in_right.at[rc, :rows], (b_s, b_r), 1 + rc, near[1 + rc])
            )
            copies.append(
                send(acc.at[theirs, :rows, SIDE + MID :], in_left.at[rc, :rows], (b_s, b_r), 3 + rc, near[3 + rc])
            )
        return copies

    def send_middle(rows):
        return send(acc.at[other, :rows, SIDE : SIDE + MID], in_mid.at[:rows], (b_s, b_r), 0, near[0])

    def folded(k):
        low = in_left[0, k] + in_left[1, k]
        high = in_right[0, k] + in_right[1, k]
        return acc[core, k, SIDE : SIDE + MID] + in_mid[k] + jnp.concatenate([low, high], axis=0)

    def keep_tails(rows):
        n = rows * WIN
        for c in range(2):
            for k in range(OWN + (rows > ROWS)):
                at = WIN * (OWN * c + k if k < OWN else ROWS)
                whole = total_t[at : at + WIN] + total_t[n + at : n + at + WIN]
                acc[c, k] = -whole if k < OWN else whole

    def keep_heads(rows):
        n = rows * MID
        for c in range(2):
            for k in range(OWN + (rows > ROWS)):
                at = MID * (OWN * c + k if k < OWN else ROWS)
                acc[c, k, SIDE : SIDE + MID] += total_h[at : at + MID] + total_h[n + at : n + at + MID]

    def lanes_of(value):
        row = jnp.sum(value, axis=0, keepdims=True)
        return row[:, :128] + row[:, 128:]

    DIAG, GROUND, R, PP, S, X = 0, 1, 2, 2 + OWN, 2 + 2 * OWN, 2 + 3 * OWN

    total_t[...] = jnp.zeros_like(total_t)
    total_h[...] = jnp.zeros_like(total_h)

    def sketch_block(j):
        block = (y + NY - j) % NY

        @pl.when(j > 0)
        def _():
            block_copy(j).wait()

        prepare(eb, pre, block)
        loop(0, 2, lambda half: sketch_tails(pre, 2 * block + half, shift, ends, total_t))

        @pl.when(j == 0)
        def _():
            loop(0, 2, lambda half: sketch_heads(pre, 2 * block + half, ends, total_h))

    loop(0, NY, sketch_block)
    keep_tails(ROWS + 1)
    borders = send_borders(OWN + 1)
    loop(2, 2 * NY, lambda c: sketch_heads(pre, (2 * y + c) % (2 * NY), ends, total_h))
    keep_heads(ROWS + 1)
    middle = send_middle(OWN + 1)
    finish(grounds)
    for j in range(8):
        for row in range(4):
            lanes = slice(128 * (row % 2), 128 * (row % 2 + 1))
            state[GROUND, 2 * j + row // 2 : 2 * j + row // 2 + 1, lanes] = gb[j, row : row + 1, :]
    finish(borders + [middle])
    state[DIAG] = folded(OWN) + state[GROUND]
    for k in range(OWN):
        state[R + k] = folded(k)
        table[core, k, SIDE : SIDE + MID] = state[R + k] / state[DIAG]

    state[PP:] = jnp.zeros_like(state[PP:])

    def iterate(it, carry):
        gamma_was, curve_was = carry
        mine = table.at[core]
        halos = []
        for rc in range(2):
            halos.append(send(mine.at[:, SIDE : 2 * SIDE], mine.at[:, SIDE + MID :], (a_s, a_r), 1 + rc, near[1 + rc]))
            halos.append(send(mine.at[:, MID : SIDE + MID], mine.at[:, :SIDE], (a_s, a_r), 3 + rc, near[3 + rc]))
        to_partner = send(mine.at[:, SIDE : SIDE + MID], mine.at[:, SIDE : SIDE + MID], (a_s, a_r), 0, near[0])
        total_t[...] = jnp.zeros_like(total_t)
        total_h[...] = jnp.zeros_like(total_h)
        energy[...] = jnp.zeros_like(energy)
        stat_s[it] = jnp.zeros_like(stat_s[it])
        for k in range(OWN):
            u = table[core, k, SIDE : SIDE + MID]
            stat_s[it, core, OWN + k : OWN + k + 1, :] = lanes_of(state[R + k] * u)
            stat_s[it, core, 2 * OWN + k : 2 * OWN + k + 1, :] = lanes_of(state[S + k] * u)
        to_partner.wait()
        for c in range(2):
            tables(table, c, tab_h, SIDE, MID)
        loop(0, NY, lambda c: gather_heads(pre, c, tab_h, first_values))
        finish(halos)
        for c in range(2):
            tables(table, c, tab_t, 0, WIN)
        loop(0, NY, lambda c: gather_tails(pre, c, tab_t, first_values, diffs, energy))

        for c in range(2):
            stat_s[it, c, :OWN, :] = energy[OWN * c : OWN * (c + 1), :]
        for k in range(OWN):
            u = table[core, k, SIDE : SIDE + MID]
            stat_s[it, core, k : k + 1, :] += lanes_of(state[GROUND] * u * u)
        slot = 2 * x + core
        copies = []
        for at in range(1, 2 * NX):
            theirs = (core + at % 2) % 2
            copies.append(
                send(stat_s.at[it, theirs], stat_x.at[it, slot], (x_s.at[it], x_r.at[it]), at - 1, along_x[at])
            )
        stat_x[it, slot] = stat_s[it, core]
        loop(0, NY - 1, lambda c: scatter_tails(c, ROWS))
        finish(copies)
        part = stat_x[it, 0]
        for j in range(1, 2 * NX):
            part = part + stat_x[it, j]
        stat_z[it, z] = part
        copies = []
        for j in range(1, NZ):
            here = stat_z.at[it, z]
            copies.append(send(here, here, (z_s.at[it], z_r.at[it]), j - 1, along_z[j - 1]))
        loop(NY - 1, NY, lambda c: scatter_tails(c, ROWS))
        keep_tails(ROWS)
        borders = send_borders(OWN)
        loop(0, NY, lambda c: scatter_heads(c, ROWS))
        keep_heads(ROWS)
        middle = send_middle(OWN)
        finish(copies)
        whole = stat_z[it, 0]
        for j in range(1, NZ):
            whole = whole + stat_z[it, j]
        totals = jnp.sum(whole, axis=1, keepdims=True)
        curve, gamma = totals[:OWN], totals[OWN : 2 * OWN]
        beta = jnp.where(it > 0, gamma / gamma_was, 0.0)
        curve = curve + 2.0 * beta * totals[2 * OWN : 3 * OWN] + beta * beta * curve_was
        alpha = gamma / curve
        finish(borders + [middle])
        for k in range(OWN):
            a = alpha[k : k + 1]
            u = table[core, k, SIDE : SIDE + MID]
            image = folded(k) + state[GROUND] * u
            b = beta[k : k + 1]
            direction = u + b * state[PP + k]
            along = image + b * state[S + k]
            state[X + k] = state[X + k] + a * direction
            state[PP + k] = direction
            state[S + k] = along
            rest = state[R + k] - a * along
            state[R + k] = rest
            table[core, k, SIDE : SIDE + MID] = rest / state[DIAG]
        return gamma, curve

    lax.fori_loop(0, ITERS, iterate, (jnp.ones((OWN, 1), F), jnp.zeros((OWN, 1), F)))

    for g in range(8):
        for k in range(OWN):
            for half in range(2):
                lanes = slice(LANES * half, LANES * (half + 1))
                tile = slice(2 * g + half, 2 * g + half + 1)
                out_s[g, k : k + 1, lanes] = state[X + k, tile, :]
                out_s[g, OWN + k : OWN + k + 1, lanes] = state[R + k, tile, :]
    copies = []
    for j in range(1, 8):
        to = (grp + j) % 8
        copies.append(send(out_s.at[to], out_r.at[grp], (o_s, o_r), j - 1, group[j - 1]))
    out_r[grp] = out_s[grp]
    finish(copies)
    for g in range(8):
        sol[OWN * g : OWN * (g + 1), :] = out_r[g, :OWN, :]
        res[OWN * g : OWN * (g + 1), :] = out_r[g, OWN : 2 * OWN, :]


def on_device(heads, tails, signs, edge_weights, ground):
    dma = lambda *shape: pltpu.SemaphoreType.DMA(shape)
    vmem = pl.BlockSpec(memory_space=pltpu.VMEM)
    out = jax.ShapeDtypeStruct((K, 512), F)
    scratch = [
        pltpu.VMEM((2, 4, 8, WIDE), F),
        pltpu.VMEM((NY, 4, 8, WIDE), F),
        pltpu.VMEM((NY, 6, 8, WIDE), F),
        pltpu.VMEM((8, 4, 128), F),
        pltpu.VMEM((2, OWN, WIN, LANES), F),
        pltpu.VMEM((2, OWN + 1, WIN, LANES), F),
        pltpu.VMEM((OWN + 1, MID, LANES), F),
        pltpu.VMEM((2, OWN + 1, SIDE, LANES), F),
        pltpu.VMEM((2, OWN + 1, SIDE, LANES), F),
        pltpu.VMEM((NY, ROWS, 8, EC), F),
        pltpu.VMEM((NY, 8, EC), F),
        pltpu.VMEM((2 * NY, 8, HALF), F),
        pltpu.VMEM((8, 128), F),
        pltpu.VMEM((2 * ROWS * WIN, LANES), BF),
        pltpu.VMEM((2 * ROWS * MID, LANES), BF),
        pltpu.VMEM((2 * (ROWS + 1) * WIN, LANES), F),
        pltpu.VMEM((2 * (ROWS + 1) * MID, LANES), F),
        pltpu.VMEM((2 + 4 * OWN, MID, LANES), F),
        pltpu.VMEM((ITERS, 2, 16, 128), F),
        pltpu.VMEM((ITERS, 2 * NX, 16, 128), F),
        pltpu.VMEM((ITERS, NZ, 16, 128), F),
        pltpu.VMEM((8, 8, 512), F),
        pltpu.VMEM((8, 8, 512), F),
    ]
    counts = [(NY - 1,), (7,), (5,), (5,), (ITERS, 2 * NX - 1), (ITERS, NZ - 1), (7,)]
    scratch += [dma(*count) for count in counts for _ in range(2)]
    return pl.pallas_call(
        kernel,
        out_shape=(out, out),
        in_specs=[vmem] * 5,
        out_specs=(vmem, vmem),
        scratch_shapes=scratch,
        compiler_params=pltpu.CompilerParams(
            collective_id=0, has_side_effects=True, vmem_limit_bytes=58 * 2**20
        ),
        name="resistances",
    )(
        heads.reshape(64, 128), tails.reshape(64, 128), edge_weights.reshape(64, 128), signs, ground.reshape(4, 128)
    )


def solution(mesh):
    in_specs = (
        P(("dom", "grp")),
        P(("dom", "grp")),
        P(None, ("dom", "grp")),
        P(("dom", "grp")),
        P(("dom", "grp")),
    )
    out_specs = (P(None, ("dom", "grp")), P(None, ("dom", "grp")))
    return jax.shard_map(
        on_device, mesh=mesh, in_specs=in_specs, out_specs=out_specs, check_vma=False
    )
```
